32 devices in a mesh: inst: 8 (over y, x, core), space: 4 (over z).
Axes of the slice: x: 2, y: 2, z: 4, core: 2. Of those that a mesh axis runs over, the one named last changes fastest.
Arguments:
- adjoint: float32 [8, 5, 16, 16, 128], P('inst', None, 'space'), may hold values from -6 to 6
- jacobian: float32 [8, 7, 5, 5, 16, 16, 128], P('inst', None, None, None, 'space'), may hold values from -4 to 4
- volume: float32 [16, 16, 128], P('space'), may hold values from 0.5 to 2
- source: float32 [8, 5, 16, 16, 128], P('inst', None, 'space'), may hold values from -6 to 6
- surface_out: float32 [5, 16, 128], P(None, 'space'), may hold values from -1 to 1
- surface_in: float32 [5, 16, 128], P(None, 'space'), may hold values from -6 to 6
- station: int32 [16, 128], P('space'), may hold values from 0 to 255
- phi: float32 [40, 256], replicated, may hold values from -0.375 to 0.375
- inv_stiff: float32 [40], replicated, may hold values from 0.5 to 8
Outputs:
- residual: float32 [8, 5, 16, 16, 128], P('inst', None, 'space')
- modal: float32 [8, 40], P('inst')
The draws below stay inside these ranges and needn't reach their ends.
All inputs are finite; a program needn't handle non-finite values.
Results may differ from the reference program's by a relative error of at most 0.000078.
Values sent between devices are 32-bit elements; how exact they have to be, the bound alone decides.
No kernel may reach another device: no remote copies, remote signals or barrier semaphores. Data moves between devices by JAX's collectives and lax.ppermute only.
A program may use at most 64 MiB of HBM per device.

```python
import math
import jax
import jax.numpy as jnp
from jax import lax

NV = 5
M = 40
NS = 256
NY = 16
NZ = 128
NT = 8
NX = 16


def plant(drawn, stream_key, least, largest):
    shape = drawn.shape
    place = [jax.random.randint(jax.random.fold_in(stream_key, axis), (), 0, shape[axis]) for axis in range(len(shape))]
    drawn = drawn.at[tuple(place)].set(least)
    longest = shape.index(max(shape))
    place[longest] = (place[longest] + 1) % shape[longest]
    return drawn.at[tuple(place)].set(largest)


def shard_levels(key, shape, cuts, least, largest):
    gain = 1.0
    for dim, shards_of in cuts:
        heights = jax.random.uniform(jax.random.fold_in(jax.random.fold_in(key, 6), dim), (shards_of,), jnp.float32, least / len(cuts), largest / len(cuts))
        gain = gain * jnp.repeat(jnp.exp(heights), shape[dim] // shards_of).reshape((-1,) + (1,) * (len(shape) - 1 - dim))
    return gain


def bell_draw(rng, shape, width, reach, cuts=(), dtype=jnp.bfloat16):
    level = shard_levels(rng, shape, cuts, -0.22, 0.18) if cuts else 1.0
    drawn = jax.random.normal(rng, shape, jnp.float32) * width * level
    return jnp.minimum(jnp.maximum(drawn, -reach), reach).astype(dtype)


def setup_inputs(seed: int = 0) -> dict:
    key_of = jax.random.split(jax.random.key(seed), 10)
    return {
        "adjoint": bell_draw(key_of[0], (NT, NV, NX, NY, NZ), 1.0, 6.0, ((0, 8), (2, 4)), jnp.float32),
        "jacobian": bell_draw(key_of[1], (NT, 7, NV, NV, NX, NY, NZ), 0.3, 4.0, ((0, 8), (4, 4)), jnp.float32),
        "volume": jnp.clip(jnp.exp(math.log(2.0) - 1.3862944 * jax.random.uniform(key_of[2], (NX, NY, NZ), jnp.float32) ** shard_levels(key_of[2], (NX, NY, NZ), ((0, 4),), -0.2, 0.2)), 0.5, 2.0),
        "source": bell_draw(key_of[3], (NT, NV, NX, NY, NZ), 1.0, 6.0, ((0, 8), (2, 4)), jnp.float32),
        "surface_out": bell_draw(key_of[4], (NV, NX, NZ), (NV * NX * NZ // NS) ** -0.5, 1.0, ((1, 4),), jnp.float32),
        "surface_in": bell_draw(key_of[5], (NV, NX, NZ), 1.0, 6.0, ((1, 4),), jnp.float32),
        "station": plant(jax.random.randint(key_of[6], (NX, NZ), 0, NS), jax.random.fold_in(key_of[6], 1), 0, NS - 1).astype(jnp.int32),
        "phi": bell_draw(key_of[7], (M, NS), NS ** -0.5, 0.375, (), jnp.float32),
        "inv_stiff": jnp.clip(jnp.exp(jax.random.uniform(key_of[8], (M,), jnp.float32, math.log(0.5), math.log(8.0))), 0.5, 8.0),
    }


def time_weights(count):
    index = jnp.arange(count)
    diff = index[:, None] - index[None, :]
    angle = jnp.pi * diff.astype(jnp.float32) / count
    parity = (1 - 2 * (diff % 2)).astype(jnp.float32)
    offdiag = diff != 0
    safe_sin = jnp.where(offdiag, jnp.sin(angle), jnp.float32(1.0))
    first = jnp.where(offdiag, 0.5 * parity * jnp.cos(angle) / safe_sin, jnp.float32(0.0))
    second = jnp.where(offdiag, -0.5 * parity / (safe_sin * safe_sin), -(count * count + 2) / 12.0)
    return first - 0.25 * second


def stencil(pair):
    blocks, lam = pair
    prod = jnp.einsum('dijxyz,ixyz->djxyz', blocks, lam, precision=lax.Precision.HIGHEST)
    flux = prod[0] + jnp.roll(prod[1], 1, axis=1) + jnp.roll(prod[2], -1, axis=1)
    flux = flux + jnp.pad(prod[3], ((0, 0), (0, 0), (1, 0), (0, 0)))[:, :, :-1]
    flux = flux + jnp.pad(prod[4], ((0, 0), (0, 0), (0, 1), (0, 0)))[:, :, 1:]
    flux = flux + jnp.pad(prod[5], ((0, 0), (0, 0), (0, 0), (1, 0)))[:, :, :, :-1]
    flux = flux + jnp.pad(prod[6], ((0, 0), (0, 0), (0, 0), (0, 1)))[:, :, :, 1:]
    return flux


def reference(adjoint, jacobian, volume, source, surface_out, surface_in, station, phi, inv_stiff):
    count = adjoint.shape[0]
    weights = time_weights(count)
    flux = lax.map(stencil, (jacobian, adjoint))
    spectral = volume[None, None] * jnp.einsum('mn,mjxyz->njxyz', weights, adjoint, precision=lax.Precision.HIGHEST)
    face = jnp.einsum('jxz,njxz->nxz', surface_out, adjoint[:, :, :, 0, :], precision=lax.Precision.HIGHEST)
    flat_station = station.reshape(-1)
    loads = jax.ops.segment_sum(face.reshape(count, -1).T, flat_station, phi.shape[1]).T
    modal = inv_stiff[None, :] * jnp.dot(loads, phi.T, precision=lax.Precision.HIGHEST)
    back = jnp.dot(modal, phi[:, flat_station], precision=lax.Precision.HIGHEST).reshape(face.shape)
    residual = flux + spectral - source
    residual = residual.at[:, :, :, 0, :].add(surface_in[None] * back[:, None])
    return residual, modal
```

```python
import functools
import math

import jax
import jax.numpy as jnp
import numpy as np
from jax import lax
from jax.experimental import pallas as pl
from jax.experimental.pallas import tpu as pltpu
from jax.sharding import PartitionSpec as P

VMEM = pl.BlockSpec(memory_space=pltpu.VMEM)
HBM = pl.BlockSpec(memory_space=pltpu.HBM)
F32 = jnp.float32


def weight_table(count):
    table = []
    for k in range(count):
        if k == 0:
            first, second = 0.0, -(count * count + 2) / 12.0
        else:
            sign = 1.0 - 2.0 * (k % 2)
            sine = math.sin(math.pi * k / count)
            first = 0.5 * sign * math.cos(math.pi * k / count) / sine
            second = -0.5 * sign / (sine * sine)
        table.append(first - 0.25 * second)
    return np.asarray(table, np.float32)


def weight_of(count, source, target):
    gap = lax.rem(source - target + count, count)
    value = jnp.float32(0.0)
    for k, entry in enumerate(weight_table(count)):
        value = jnp.where(gap == k, jnp.float32(entry), value)
    return value


def prep_kernel(
    lam_in, source_in, volume_in, inward_in, outward_in, station_in, phi_in, stiff_in, jac,
    near, wrap, packed, modes, lam, source, volume, inward,
    block, outward, station, phi, inv_stiff, sem,
):
    nv, nx, ny, nz = lam.shape[1:]
    odd = lax.rem(lax.axis_index("space"), 2)
    sides = (odd, 1 - odd)
    moves = [(station_in, station), (phi_in, phi), (stiff_in, inv_stiff), (outward_in, outward), (lam_in, lam)]
    for slot, minus in enumerate(sides):
        moves.append((jac.at[0, 1 + minus, :, :, (nx - 1) * (1 - minus)], block.at[slot]))
    moves += [(source_in, source), (volume_in, volume), (inward_in, inward)]
    copies = [pltpu.make_async_copy(src, dst, sem.at[i]) for i, (src, dst) in enumerate(moves)]
    for copy in copies:
        copy.start()
    modes_k, stations = phi.shape
    copies[0].wait()
    copies[1].wait()
    full = phi[...]
    high = full.astype(jnp.bfloat16)
    rest = full - high.astype(F32)
    mid = rest.astype(jnp.bfloat16)
    low = (rest - mid.astype(F32)).astype(jnp.bfloat16)
    rows = lax.broadcasted_iota(jnp.int32, (stations, nz), 0)
    for x in range(nx):
        hot = (rows == station[x : x + 1, :]).astype(F32).astype(jnp.bfloat16)
        modes[x] = (
            jnp.dot(low, hot, preferred_element_type=F32)
            + jnp.dot(mid, hot, preferred_element_type=F32)
            + jnp.dot(high, hot, preferred_element_type=F32)
        )
    for copy in copies[2:5]:
        copy.wait()
    share = jnp.zeros((modes_k, nz), F32)
    for x in range(nx):
        face = outward[0, x : x + 1, :] * lam[0, 0, x, 0:1, :]
        for j in range(1, nv):
            face = face + outward[j, x : x + 1, :] * lam[0, j, x, 0:1, :]
        share = share + modes[x] * face
    row = lax.broadcasted_iota(jnp.int32, (modes_k, modes_k), 0)
    lane = lax.broadcasted_iota(jnp.int32, (modes_k, modes_k), 1)
    stiff = jnp.sum(jnp.where(row == lane, inv_stiff[...], 0.0), axis=1, keepdims=True)
    column = jnp.sum(share, axis=1, keepdims=True) * stiff
    tile_lane = lax.broadcasted_iota(jnp.int32, (8, nz), 1)
    tile = jnp.zeros((8, nz), F32)
    for group in range(modes_k // 8):
        tile = jnp.where(tile_lane == group, column[8 * group : 8 * group + 8], tile)
    packed[...] = tile
    near[nv * ny :, :] = tile
    wrap[nv * ny :, :] = tile
    for slot, (minus, out) in enumerate(zip(sides, (near, wrap))):
        copies[5 + slot].wait()
        cells = lam[0, :, (nx - 1) * (1 - minus)]
        for j in range(nv):
            total = block[slot, 0, j] * cells[0]
            for i in range(1, nv):
                total = total + block[slot, i, j] * cells[i]
            out[j * ny : (j + 1) * ny, :] = total
    for copy in copies[7:]:
        copy.wait()


def share_kernel(masks, *refs):
    held, out = refs[:-1], refs[-1]
    count = lax.axis_size("inst")
    me = lax.axis_index("inst")
    total = None
    for mask, block in zip(masks, held):
        term = weight_of(count, me ^ mask, me ^ 1) * block[0]
        total = term if total is None else total + term
    out[0] = total


def own_kernel(masks, partial, volume, *refs):
    held, out = refs[:-1], refs[-1]
    count = lax.axis_size("inst")
    me = lax.axis_index("inst")
    total = None
    for mask, block in zip(masks, held):
        term = weight_of(count, me ^ mask, me) * block[0]
        total = term if total is None else total + term
    out[0] = volume[...][None] * total + partial[0]


def flux_kernel(lam, source, jac, out):
    nv, nx, ny, nz = lam.shape[1:]
    y = lax.broadcasted_iota(jnp.int32, (ny, nz), 0)
    z = lax.broadcasted_iota(jnp.int32, (ny, nz), 1)

    def product(d, j, x):
        total = jac[0, d, 0, j, x] * lam[0, 0, x]
        for i in range(1, nv):
            total = total + jac[0, d, i, j, x] * lam[0, i, x]
        return total

    for j in range(nv):
        for x in range(nx):
            total = product(0, j, x) - source[0, j, x]
            if x > 0:
                total = total + product(1, j, x - 1)
            if x < nx - 1:
                total = total + product(2, j, x + 1)
            total = total + jnp.where(y == 0, 0.0, pltpu.roll(product(3, j, x), 1, 0))
            total = total + jnp.where(y == ny - 1, 0.0, pltpu.roll(product(4, j, x), ny - 1, 0))
            total = total + jnp.where(z == 0, 0.0, pltpu.roll(product(5, j, x), 1, 1))
            total = total + jnp.where(z == nz - 1, 0.0, pltpu.roll(product(6, j, x), nz - 1, 1))
            out[0, j, x] = total


def final_kernel(partial, volume, mix, near, wrap, modal_tile, modes, surface_in, out, modal):
    nv, nx, ny, nz = partial.shape[1:]
    groups = modal.shape[1] // 8
    odd = lax.rem(lax.axis_index("space"), 2)
    tile = modal_tile[...]
    columns = [tile[:, group : group + 1] for group in range(groups)]
    for group, column in enumerate(columns):
        row = lax.broadcasted_iota(jnp.int32, (8, 8 * groups), 0)
        lane = lax.broadcasted_iota(jnp.int32, (8, 8 * groups), 1)
        piece = jnp.sum(jnp.where(lane == row + 8 * group, column, 0.0), axis=0, keepdims=True)
        line = piece if group == 0 else line + piece
    modal[...] = line
    low = lax.broadcasted_iota(jnp.int32, (ny, nz), 0) == 0
    is_odd = odd == 1
    for x in range(nx):
        back = jnp.zeros((8, nz), F32)
        for group, column in enumerate(columns):
            back = back + modes[x, 8 * group : 8 * group + 8, :] * column
        back = jnp.sum(back, axis=0, keepdims=True)
        for j in range(nv):
            value = partial[0, j, x] + volume[x] * mix[0, j, x]
            rows = pl.ds(j * ny, ny)
            if x == 0:
                value = value + jnp.where(is_odd, near[rows, :], wrap[rows, :])
            if x == nx - 1:
                value = value + jnp.where(is_odd, wrap[rows, :], near[rows, :])
            out[0, j, x] = value + jnp.where(low, surface_in[j, x : x + 1, :] * back, 0.0)


def body(adjoint, jacobian, volume, source, surface_out, surface_in, station, phi, inv_stiff):
    count, slabs = lax.axis_size("inst"), lax.axis_size("space")
    nv, nx, ny, nz = adjoint.shape[1:]
    modes_k = phi.shape[0]

    def swap(value, axis, mask):
        size = lax.axis_size(axis)
        return lax.ppermute(value, axis, [(i, i ^ mask) for i in range(size)])

    def like(array):
        return jax.ShapeDtypeStruct(array.shape, F32)

    masks = tuple(range(0, count, 2))
    foreign = [swap(adjoint, "inst", mask) for mask in masks[1:]]
    rows = nv * ny + 8
    whole = (adjoint, source, volume, surface_in, surface_out, station, phi, inv_stiff.reshape(1, modes_k), jacobian)
    near, wrap, packed, modes, lam, src, vol, inward = pl.pallas_call(
        prep_kernel,
        out_shape=(
            pltpu.VMEM((rows, nz), F32),
            pltpu.VMEM((rows, nz), F32),
            pltpu.VMEM((8, nz), F32),
            pltpu.VMEM((nx, modes_k, nz), F32),
            pltpu.VMEM(adjoint.shape, F32),
            pltpu.VMEM(source.shape, F32),
            pltpu.VMEM(volume.shape, F32),
            pltpu.VMEM(surface_in.shape, F32),
        ),
        in_specs=[HBM] * 9,
        out_specs=(VMEM,) * 8,
        scratch_shapes=[
            pltpu.VMEM((2, nv, nv, ny, nz), F32),
            pltpu.VMEM(surface_out.shape, F32),
            pltpu.VMEM(station.shape, station.dtype),
            pltpu.VMEM(phi.shape, F32),
            pltpu.VMEM((1, modes_k), F32),
            pltpu.SemaphoreType.DMA((10,)),
        ],
        compiler_params=pltpu.CompilerParams(vmem_limit_bytes=8 * 2**20),
        name="prep",
    )(*(pltpu.with_memory_space_constraint(value, pltpu.HBM) for value in whole))
    wrap_in = lax.ppermute(wrap, "space", [(i, (((i + 1) ^ 1) - 1) % slabs) for i in range(slabs)])
    near_in = swap(near, "space", 1)
    if slabs == 4:
        far_in = swap(packed, "space", 2)
        tile = (packed + near_in[nv * ny :]) + (wrap_in[nv * ny :] + far_in)
    else:
        tile = packed + near_in[nv * ny :]
        step = 2
        while step < slabs:
            tile = tile + swap(tile, "space", step)
            step *= 2
    partial = pl.pallas_call(
        flux_kernel,
        out_shape=like(adjoint),
        in_specs=[VMEM] * 3,
        out_specs=VMEM,
        compiler_params=pltpu.CompilerParams(vmem_limit_bytes=16 * 2**20),
        cost_estimate=pl.CostEstimate(flops=2 * jacobian.size, bytes_accessed=4 * jacobian.size, transcendentals=0),
        name="flux",
    )(lam, src, jacobian)
    held = [lam] + foreign
    share = pl.pallas_call(
        functools.partial(share_kernel, masks),
        out_shape=like(adjoint),
        in_specs=[VMEM] * len(masks),
        out_specs=VMEM,
        compiler_params=pltpu.CompilerParams(vmem_limit_bytes=8 * 2**20),
        name="share",
    )(*held)
    mix = swap(share, "inst", 1)
    partial = pl.pallas_call(
        functools.partial(own_kernel, masks),
        out_shape=like(adjoint),
        in_specs=[VMEM] * (2 + len(masks)),
        out_specs=VMEM,
        compiler_params=pltpu.CompilerParams(vmem_limit_bytes=8 * 2**20),
        name="own",
    )(partial, vol, *held)
    residual, modal = pl.pallas_call(
        final_kernel,
        out_shape=(like(adjoint), jax.ShapeDtypeStruct((1, modes_k), F32)),
        in_specs=[VMEM] * 8,
        out_specs=(VMEM, VMEM),
        compiler_params=pltpu.CompilerParams(vmem_limit_bytes=8 * 2**20),
        name="final",
    )(partial, vol, mix, near_in, wrap_in, tile, modes, inward)
    return residual, modal


def solution(mesh):
    placed = (
        P("inst", None, "space", None, None),
        P("inst", None, None, None, "space", None, None),
        P("space", None, None),
        P("inst", None, "space", None, None),
        P(None, "space", None),
        P(None, "space", None),
        P("space", None),
        P(),
        P(),
    )
    return jax.shard_map(
        body,
        mesh=mesh,
        in_specs=placed,
        out_specs=(P("inst", None, "space", None, None), P("inst", None)),
        check_vma=False,
    )
```

```python
import functools
import math

import jax
import jax.numpy as jnp
import numpy as np
from jax import lax
from jax.experimental import pallas as pl
from jax.experimental.pallas import tpu as pltpu
from jax.sharding import PartitionSpec as P

VMEM = pl.BlockSpec(memory_space=pltpu.VMEM)
HBM = pl.BlockSpec(memory_space=pltpu.HBM)
F32 = jnp.float32


def weight_table(count):
    table = []
    for k in range(count):
        if k == 0:
            first, second = 0.0, -(count * count + 2) / 12.0
        else:
            sign = 1.0 - 2.0 * (k % 2)
            sine = math.sin(math.pi * k / count)
            first = 0.5 * sign * math.cos(math.pi * k / count) / sine
            second = -0.5 * sign / (sine * sine)
        table.append(first - 0.25 * second)
    return np.asarray(table, np.float32)


def weight_of(count, source, target):
    gap = lax.rem(source - target + count, count)
    value = jnp.float32(0.0)
    for k, entry in enumerate(weight_table(count)):
        value = jnp.where(gap == k, jnp.float32(entry), value)
    return value


def prep_kernel(targets, sibling, lam_in, outward_in, station_in, phi_in, stiff_in, jac, near, wrap, packed, modes, lam, *refs):
    blends, (planes, outward, station, phi, inv_stiff, sem) = refs[: len(targets)], refs[len(targets) :]
    nv, nx, ny, nz = lam.shape[1:]
    count = lax.axis_size("inst")
    me = lax.axis_index("inst")
    odd = lax.rem(lax.axis_index("space"), 2)
    sides = (1 - odd, odd)
    moves = [(station_in, station), (phi_in, phi), (lam_in, lam), (outward_in, outward), (stiff_in, inv_stiff)]
    for slot, minus in enumerate(sides):
        moves.append((jac.at[0, 1 + minus, :, :, (nx - 1) * (1 - minus)], planes.at[slot]))
    copies = [pltpu.make_async_copy(src, dst, sem.at[i]) for i, (src, dst) in enumerate(moves)]
    for copy in copies:
        copy.start()
    modes_k, stations = phi.shape
    copies[0].wait()
    copies[1].wait()
    full = phi[...]
    high = full.astype(jnp.bfloat16)
    rest = full - high.astype(F32)
    mid = rest.astype(jnp.bfloat16)
    low = (rest - mid.astype(F32)).astype(jnp.bfloat16)
    rows = lax.broadcasted_iota(jnp.int32, (stations, nz), 0)
    for x in range(nx):
        hot = (rows == station[x : x + 1, :]).astype(F32).astype(jnp.bfloat16)
        modes[x] = (
            jnp.dot(low, hot, preferred_element_type=F32)
            + jnp.dot(mid, hot, preferred_element_type=F32)
            + jnp.dot(high, hot, preferred_element_type=F32)
        )
    for copy in copies[2:5]:
        copy.wait()
    share = jnp.zeros((modes_k, nz), F32)
    for x in range(nx):
        face = outward[0, x : x + 1, :] * lam[0, 0, x, 0:1, :]
        for j in range(1, nv):
            face = face + outward[j, x : x + 1, :] * lam[0, j, x, 0:1, :]
        share = share + modes[x] * face
    row = lax.broadcasted_iota(jnp.int32, (modes_k, modes_k), 0)
    lane = lax.broadcasted_iota(jnp.int32, (modes_k, modes_k), 1)
    stiff = jnp.sum(jnp.where(row == lane, inv_stiff[...], 0.0), axis=1, keepdims=True)
    column = jnp.sum(share, axis=1, keepdims=True) * stiff
    tile_lane = lax.broadcasted_iota(jnp.int32, (8, nz), 1)
    tile = jnp.zeros((8, nz), F32)
    for group in range(modes_k // 8):
        tile = jnp.where(tile_lane == group, column[8 * group : 8 * group + 8], tile)
    packed[...] = tile
    near[nv * ny :, :] = tile
    wrap[nv * ny :, :] = tile
    for mask, blend in zip(targets, blends):
        own = weight_of(count, me, me ^ mask)
        other = weight_of(count, me ^ 1, me ^ mask)
        blend[0] = own * lam[0] + other * sibling[0]
    for slot, (minus, out) in enumerate(zip(sides, (wrap, near))):
        copies[5 + slot].wait()
        cells = lam[0, :, (nx - 1) * (1 - minus)]
        for j in range(nv):
            total = planes[slot, 0, j] * cells[0]
            for i in range(1, nv):
                total = total + planes[slot, i, j] * cells[i]
            out[j * ny : (j + 1) * ny, :] = total


def mix_of(masks, blocks, target):
    count = lax.axis_size("inst")
    me = lax.axis_index("inst")
    total = None
    for mask, block in zip(masks, blocks):
        term = weight_of(count, me ^ mask, me ^ target) * block[0]
        total = term if total is None else total + term
    return total


def share_kernel(masks, *refs):
    refs[-1][0] = mix_of(masks, refs[:-1], 1)


def own_kernel(masks, partial, volume, *refs):
    refs[-1][0] = volume[...][None] * mix_of(masks, refs[:-1], 0) + partial[0]


def flux_kernel(lam, source, jac, out):
    nv, nx, ny, nz = lam.shape[1:]
    y = lax.broadcasted_iota(jnp.int32, (ny, nz), 0)
    z = lax.broadcasted_iota(jnp.int32, (ny, nz), 1)

    def product(d, j, x):
        total = jac[0, d, 0, j, x] * lam[0, 0, x]
        for i in range(1, nv):
            total = total + jac[0, d, i, j, x] * lam[0, i, x]
        return total

    for j in range(nv):
        for x in range(nx):
            total = product(0, j, x) - source[0, j, x]
            if x > 0:
                total = total + product(1, j, x - 1)
            if x < nx - 1:
                total = total + product(2, j, x + 1)
            total = total + jnp.where(y == 0, 0.0, pltpu.roll(product(3, j, x), 1, 0))
            total = total + jnp.where(y == ny - 1, 0.0, pltpu.roll(product(4, j, x), ny - 1, 0))
            total = total + jnp.where(z == 0, 0.0, pltpu.roll(product(5, j, x), 1, 1))
            total = total + jnp.where(z == nz - 1, 0.0, pltpu.roll(product(6, j, x), nz - 1, 1))
            out[0, j, x] = total


def final_kernel(partial, volume, near, wrap, modal_tile, modes, surface_in, *refs):
    mixes, (out, modal) = refs[:-2], refs[-2:]
    nv, nx, ny, nz = partial.shape[1:]
    groups = modal.shape[1] // 8
    odd = lax.rem(lax.axis_index("space"), 2)
    tile = modal_tile[...]
    columns = [tile[:, group : group + 1] for group in range(groups)]
    for group, column in enumerate(columns):
        row = lax.broadcasted_iota(jnp.int32, (8, 8 * groups), 0)
        lane = lax.broadcasted_iota(jnp.int32, (8, 8 * groups), 1)
        piece = jnp.sum(jnp.where(lane == row + 8 * group, column, 0.0), axis=0, keepdims=True)
        line = piece if group == 0 else line + piece
    modal[...] = line
    low = lax.broadcasted_iota(jnp.int32, (ny, nz), 0) == 0
    is_odd = odd == 1
    for x in range(nx):
        back = jnp.zeros((8, nz), F32)
        for group, column in enumerate(columns):
            back = back + modes[x, 8 * group : 8 * group + 8, :] * column
        back = jnp.sum(back, axis=0, keepdims=True)
        for j in range(nv):
            mixed = mixes[0][0, j, x]
            for mix in mixes[1:]:
                mixed = mixed + mix[0, j, x]
            value = partial[0, j, x] + volume[x] * mixed
            rows = pl.ds(j * ny, ny)
            if x == 0:
                value = value + jnp.where(is_odd, near[rows, :], wrap[rows, :])
            if x == nx - 1:
                value = value + jnp.where(is_odd, wrap[rows, :], near[rows, :])
            out[0, j, x] = value + jnp.where(low, surface_in[j, x : x + 1, :] * back, 0.0)


def body(adjoint, jacobian, volume, source, surface_out, surface_in, station, phi, inv_stiff):
    count, slabs = lax.axis_size("inst"), lax.axis_size("space")
    nv, nx, ny, nz = adjoint.shape[1:]
    modes_k = phi.shape[0]

    def swap(value, axis, mask):
        size = lax.axis_size(axis)
        return lax.ppermute(value, axis, [(i, i ^ mask) for i in range(size)])

    def like(array):
        return jax.ShapeDtypeStruct(array.shape, F32)

    def fast(array):
        return pltpu.with_memory_space_constraint(array, pltpu.VMEM)

    masks = [mask for mask in range(2, count, 2) if mask & (mask - 1) == 0]
    targets = [mask for mask in range(2, count, 2) if mask & (mask - 1)]
    sibling = swap(adjoint, "inst", 1)
    foreign = [swap(adjoint, "inst", mask) for mask in masks]
    rows = nv * ny + 8
    whole = (adjoint, surface_out, station, phi, inv_stiff.reshape(1, modes_k), jacobian)
    near, wrap, packed, modes, lam, *blends = pl.pallas_call(
        functools.partial(prep_kernel, targets),
        out_shape=(
            pltpu.VMEM((rows, nz), F32),
            pltpu.VMEM((rows, nz), F32),
            pltpu.VMEM((8, nz), F32),
            pltpu.VMEM((nx, modes_k, nz), F32),
            pltpu.VMEM(adjoint.shape, F32),
        )
        + (pltpu.VMEM(adjoint.shape, F32),) * len(targets),
        in_specs=[VMEM] + [HBM] * len(whole),
        out_specs=(VMEM,) * (5 + len(targets)),
        scratch_shapes=[
            pltpu.VMEM((2, nv, nv, ny, nz), F32),
            pltpu.VMEM(surface_out.shape, F32),
            pltpu.VMEM(station.shape, station.dtype),
            pltpu.VMEM(phi.shape, F32),
            pltpu.VMEM((1, modes_k), F32),
            pltpu.SemaphoreType.DMA((7,)),
        ],
        compiler_params=pltpu.CompilerParams(vmem_limit_bytes=8 * 2**20),
        name="prep",
    )(sibling, *(pltpu.with_memory_space_constraint(value, pltpu.HBM) for value in whole))
    blends = [swap(blend, "inst", mask) for mask, blend in zip(targets, blends)]
    wrap_in = lax.ppermute(wrap, "space", [(i, (((i + 1) ^ 1) - 1) % slabs) for i in range(slabs)])
    near_in = swap(near, "space", 1)
    if slabs == 4:
        far_in = swap(packed, "space", 2)
        tile = (packed + near_in[nv * ny :]) + (wrap_in[nv * ny :] + far_in)
    else:
        tile = packed + near_in[nv * ny :]
        step = 2
        while step < slabs:
            tile = tile + swap(tile, "space", step)
            step *= 2
    partial = pl.pallas_call(
        flux_kernel,
        out_shape=like(adjoint),
        in_specs=[VMEM] * 3,
        out_specs=VMEM,
        compiler_params=pltpu.CompilerParams(vmem_limit_bytes=16 * 2**20),
        cost_estimate=pl.CostEstimate(flops=2 * jacobian.size, bytes_accessed=4 * jacobian.size, transcendentals=0),
        name="flux",
    )(lam, fast(source), fast(jacobian))
    share = pl.pallas_call(
        functools.partial(share_kernel, masks),
        out_shape=like(adjoint),
        in_specs=[VMEM] * len(masks),
        out_specs=VMEM,
        compiler_params=pltpu.CompilerParams(vmem_limit_bytes=8 * 2**20),
        name="share",
    )(*foreign)
    mixes = [swap(share, "inst", 1)] + blends
    vol = fast(volume)
    held = [lam, sibling] + foreign
    partial = pl.pallas_call(
        functools.partial(own_kernel, [0, 1] + masks),
        out_shape=like(adjoint),
        in_specs=[VMEM] * (2 + len(held)),
        out_specs=VMEM,
        compiler_params=pltpu.CompilerParams(vmem_limit_bytes=8 * 2**20),
        name="own",
    )(partial, vol, *held)
    residual, modal = pl.pallas_call(
        final_kernel,
        out_shape=(like(adjoint), jax.ShapeDtypeStruct((1, modes_k), F32)),
        in_specs=[VMEM] * (7 + len(mixes)),
        out_specs=(VMEM, VMEM),
        compiler_params=pltpu.CompilerParams(vmem_limit_bytes=8 * 2**20),
        name="final",
    )(partial, vol, near_in, wrap_in, tile, modes, fast(surface_in), *mixes)
    return residual, modal


def solution(mesh):
    placed = (
        P("inst", None, "space", None, None),
        P("inst", None, None, None, "space", None, None),
        P("space", None, None),
        P("inst", None, "space", None, None),
        P(None, "space", None),
        P(None, "space", None),
        P("space", None),
        P(),
        P(),
    )
    return jax.shard_map(
        body,
        mesh=mesh,
        in_specs=placed,
        out_specs=(P("inst", None, "space", None, None), P("inst", None)),
        check_vma=False,
    )
```

```python
import functools
import math

import jax
import jax.numpy as jnp
import numpy as np
from jax import lax
from jax.experimental import pallas as pl
from jax.experimental.pallas import tpu as pltpu
from jax.sharding import PartitionSpec as P

VMEM = pl.BlockSpec(memory_space=pltpu.VMEM)
SMEM = pl.BlockSpec(memory_space=pltpu.SMEM)
F32 = jnp.float32
SMALL = pl.CostEstimate(flops=0, bytes_accessed=0, transcendentals=0)


def weight_table(count):
    table = []
    for k in range(count):
        if k == 0:
            first, second = 0.0, -(count * count + 2) / 12.0
        else:
            sign = 1.0 - 2.0 * (k % 2)
            sine = math.sin(math.pi * k / count)
            first = 0.5 * sign * math.cos(math.pi * k / count) / sine
            second = -0.5 * sign / (sine * sine)
        table.append(first - 0.25 * second)
    return np.asarray(table, np.float32)


def weight_of(count, source, target):
    gap = lax.rem(source - target + count, count)
    value = jnp.float32(0.0)
    for k, entry in enumerate(weight_table(count)):
        value = jnp.where(gap == k, jnp.float32(entry), value)
    return value


def table_kernel(out):
    count = lax.axis_size("inst")
    me = lax.axis_index("inst")
    for target in range(2):
        for mask in range(count):
            out[target, mask] = weight_of(count, me ^ mask, me ^ target)


def prep_kernel(targets, token, sibling, lam, outward, station, phi, inv_stiff, jac, near, wrap, packed, modes, *blends):
    nv, nx, ny, nz = lam.shape[1:]
    count = lax.axis_size("inst")
    me = lax.axis_index("inst")
    odd = lax.rem(lax.axis_index("space"), 2)
    for mask, blend in zip(targets, blends):
        own = weight_of(count, me, me ^ mask)
        other = weight_of(count, me ^ 1, me ^ mask)
        blend[0] = own * lam[0] + other * sibling[0]
    for minus, out in ((1 - odd, wrap), (odd, near)):
        plane = (nx - 1) * (1 - minus)
        for j in range(nv):
            total = jac[0, 1 + minus, 0, j, plane] * lam[0, 0, plane]
            for i in range(1, nv):
                total = total + jac[0, 1 + minus, i, j, plane] * lam[0, i, plane]
            out[j * ny : (j + 1) * ny, :] = total
    modes_k, stations = phi.shape
    full = phi[...]
    high = full.astype(jnp.bfloat16)
    rest = full - high.astype(F32)
    mid = rest.astype(jnp.bfloat16)
    low = (rest - mid.astype(F32)).astype(jnp.bfloat16)
    rows = lax.broadcasted_iota(jnp.int32, (stations, nz), 0)
    share = jnp.zeros((modes_k, nz), F32)
    for x in range(nx):
        hot = (rows == station[x : x + 1, :]).astype(F32).astype(jnp.bfloat16)
        at_face = (
            jnp.dot(low, hot, preferred_element_type=F32)
            + jnp.dot(mid, hot, preferred_element_type=F32)
            + jnp.dot(high, hot, preferred_element_type=F32)
        )
        modes[x] = at_face
        face = outward[0, x : x + 1, :] * lam[0, 0, x, 0:1, :]
        for j in range(1, nv):
            face = face + outward[j, x : x + 1, :] * lam[0, j, x, 0:1, :]
        share = share + at_face * face
    row = lax.broadcasted_iota(jnp.int32, (modes_k, modes_k), 0)
    lane = lax.broadcasted_iota(jnp.int32, (modes_k, modes_k), 1)
    stiff = jnp.sum(jnp.where(row == lane, inv_stiff[...], 0.0), axis=1, keepdims=True)
    column = jnp.sum(share, axis=1, keepdims=True) * stiff
    tile_lane = lax.broadcasted_iota(jnp.int32, (8, nz), 1)
    tile = jnp.zeros((8, nz), F32)
    for group in range(modes_k // 8):
        tile = jnp.where(tile_lane == group, column[8 * group : 8 * group + 8], tile)
    packed[...] = tile
    near[nv * ny :, :] = tile
    wrap[nv * ny :, :] = tile


def mix_of(masks, blocks, target):
    count = lax.axis_size("inst")
    me = lax.axis_index("inst")
    total = None
    for mask, block in zip(masks, blocks):
        term = weight_of(count, me ^ mask, me ^ target) * block[0]
        total = term if total is None else total + term
    return total


def share_kernel(masks, after, *refs):
    refs[-1][0] = mix_of(masks, refs[:-1], 1)


def own_kernel(masks, partial, volume, wrap, *refs):
    nv, nx, ny, nz = partial.shape[1:]
    held, blends, out = refs[: len(masks)], refs[len(masks) : -1], refs[-1]
    total = mix_of(masks, held, 0)
    for blend in blends:
        total = total + blend[0]
    out[0] = volume[...][None] * total + partial[0]
    plane = (nx - 1) * lax.rem(lax.axis_index("space"), 2)
    for j in range(nv):
        out[0, j, plane] = out[0, j, plane] + wrap[j * ny : (j + 1) * ny, :]


def flux_kernel(lam, source, jac, out):
    nv, nx, ny, nz = lam.shape[1:]
    y = lax.broadcasted_iota(jnp.int32, (ny, nz), 0)
    z = lax.broadcasted_iota(jnp.int32, (ny, nz), 1)

    def product(d, j, x):
        total = jac[0, d, 0, j, x] * lam[0, 0, x]
        for i in range(1, nv):
            total = total + jac[0, d, i, j, x] * lam[0, i, x]
        return total

    for j in range(nv):
        for x in range(nx):
            total = product(0, j, x) - source[0, j, x]
            if x > 0:
                total = total + product(1, j, x - 1)
            if x < nx - 1:
                total = total + product(2, j, x + 1)
            total = total + jnp.where(y == 0, 0.0, pltpu.roll(product(3, j, x), 1, 0))
            total = total + jnp.where(y == ny - 1, 0.0, pltpu.roll(product(4, j, x), ny - 1, 0))
            total = total + jnp.where(z == 0, 0.0, pltpu.roll(product(5, j, x), 1, 1))
            total = total + jnp.where(z == nz - 1, 0.0, pltpu.roll(product(6, j, x), nz - 1, 1))
            out[0, j, x] = total


def final_kernel(partial, volume, near, modes, surface_in, mix, *refs):
    tiles, (out, modal) = refs[:-2], refs[-2:]
    nv, nx, ny, nz = partial.shape[1:]
    groups = modal.shape[1] // 8
    even = lax.rem(lax.axis_index("space"), 2) == 0
    tile = sum(ref[ref.shape[0] - 8 :, :] for ref in tiles)
    columns = [tile[:, group : group + 1] for group in range(groups)]
    line = None
    for group, column in enumerate(columns):
        row = lax.broadcasted_iota(jnp.int32, (8, 8 * groups), 0)
        lane = lax.broadcasted_iota(jnp.int32, (8, 8 * groups), 1)
        piece = jnp.sum(jnp.where(lane == row + 8 * group, column, 0.0), axis=0, keepdims=True)
        line = piece if line is None else line + piece
    modal[...] = line
    low = lax.broadcasted_iota(jnp.int32, (ny, nz), 0) == 0
    for x in range(nx):
        back = jnp.zeros((8, nz), F32)
        for group, column in enumerate(columns):
            back = back + modes[x, 8 * group : 8 * group + 8, :] * column
        back = jnp.sum(back, axis=0, keepdims=True)
        for j in range(nv):
            value = partial[0, j, x] + volume[x] * mix[0, j, x]
            if x == 0 or x == nx - 1:
                border = near[j * ny : (j + 1) * ny, :]
                value = value + jnp.where(even if x else jnp.logical_not(even), border, 0.0)
            out[0, j, x] = value + jnp.where(low, surface_in[j, x : x + 1, :] * back, 0.0)


def body(adjoint, jacobian, volume, source, surface_out, surface_in, station, phi, inv_stiff):
    count, slabs = lax.axis_size("inst"), lax.axis_size("space")
    nv, nx, ny, nz = adjoint.shape[1:]
    modes_k = phi.shape[0]

    def swap(value, axis, mask):
        size = lax.axis_size(axis)
        return lax.ppermute(value, axis, [(i, i ^ mask) for i in range(size)])

    def like(array):
        return jax.ShapeDtypeStruct(array.shape, F32)

    def fast(array):
        return pltpu.with_memory_space_constraint(array, pltpu.VMEM)

    masks = [mask for mask in range(2, count, 2) if mask & (mask - 1) == 0]
    targets = [mask for mask in range(2, count, 2) if mask & (mask - 1)]
    sibling = swap(adjoint, "inst", 1)
    foreign = [swap(adjoint, "inst", mask) for mask in masks]
    rows = nv * ny + 8
    lam, jac = fast(adjoint), fast(jacobian)
    weights = pl.pallas_call(
        table_kernel,
        out_shape=pltpu.SMEM((2, count), F32),
        out_specs=SMEM,
        cost_estimate=pl.CostEstimate(flops=2**31, bytes_accessed=0, transcendentals=0),
        name="table",
    )()
    near, wrap, packed, modes, *blends = pl.pallas_call(
        functools.partial(prep_kernel, targets),
        out_shape=(
            pltpu.VMEM((rows, nz), F32),
            pltpu.VMEM((rows, nz), F32),
            pltpu.VMEM((8, nz), F32),
            pltpu.VMEM((nx, modes_k, nz), F32),
        )
        + (pltpu.VMEM(adjoint.shape, F32),) * len(targets),
        in_specs=[SMEM] + [VMEM] * 7,
        out_specs=(VMEM,) * (4 + len(targets)),
        compiler_params=pltpu.CompilerParams(vmem_limit_bytes=8 * 2**20),
        name="prep",
    )(weights, sibling, lam, fast(surface_out), fast(station), fast(phi), fast(inv_stiff.reshape(1, modes_k)), jac)
    blends = [swap(blend, "inst", mask) for mask, blend in zip(targets, blends)]
    wrap_in = lax.ppermute(wrap, "space", [(i, (((i + 1) ^ 1) - 1) % slabs) for i in range(slabs)])
    near_in = swap(near, "space", 1)
    if slabs == 4:
        tiles = [packed, near_in, wrap_in, swap(packed, "space", 2)]
    else:
        tile = packed + near_in[nv * ny :]
        step = 2
        while step < slabs:
            tile = tile + swap(tile, "space", step)
            step *= 2
        tiles = [tile]
    partial = pl.pallas_call(
        flux_kernel,
        out_shape=like(adjoint),
        in_specs=[VMEM] * 3,
        out_specs=VMEM,
        compiler_params=pltpu.CompilerParams(vmem_limit_bytes=16 * 2**20),
        cost_estimate=pl.CostEstimate(flops=2 * jacobian.size, bytes_accessed=4 * jacobian.size, transcendentals=0),
        name="flux",
    )(lam, fast(source), jac)
    share = pl.pallas_call(
        functools.partial(share_kernel, masks),
        out_shape=like(adjoint),
        in_specs=[pl.BlockSpec(memory_space=pl.ANY)] + [VMEM] * len(masks),
        out_specs=VMEM,
        compiler_params=pltpu.CompilerParams(vmem_limit_bytes=8 * 2**20),
        cost_estimate=SMALL,
        name="share",
    )(partial, *foreign)
    mix = swap(share, "inst", 1)
    vol = fast(volume)
    held = [lam, sibling] + foreign
    partial = pl.pallas_call(
        functools.partial(own_kernel, [0, 1] + masks),
        out_shape=like(adjoint),
        in_specs=[VMEM] * (3 + len(held) + len(blends)),
        out_specs=VMEM,
        compiler_params=pltpu.CompilerParams(vmem_limit_bytes=8 * 2**20),
        cost_estimate=pl.CostEstimate(flops=2**31, bytes_accessed=0, transcendentals=0),
        name="own",
    )(partial, vol, wrap_in, *held, *blends)
    residual, modal = pl.pallas_call(
        final_kernel,
        out_shape=(like(adjoint), jax.ShapeDtypeStruct((1, modes_k), F32)),
        in_specs=[VMEM] * (6 + len(tiles)),
        out_specs=(VMEM, VMEM),
        compiler_params=pltpu.CompilerParams(vmem_limit_bytes=8 * 2**20),
        name="final",
    )(partial, vol, near_in, modes, fast(surface_in), mix, *tiles)
    return residual, modal


def solution(mesh):
    placed = (
        P("inst", None, "space", None, None),
        P("inst", None, None, None, "space", None, None),
        P("space", None, None),
        P("inst", None, "space", None, None),
        P(None, "space", None),
        P(None, "space", None),
        P("space", None),
        P(),
        P(),
    )
    return jax.shard_map(
        body,
        mesh=mesh,
        in_specs=placed,
        out_specs=(P("inst", None, "space", None, None), P("inst", None)),
        check_vma=False,
    )
```

```python
import functools
import math

import jax
import jax.numpy as jnp
import numpy as np
from jax import lax
from jax.experimental import pallas as pl
from jax.experimental.pallas import tpu as pltpu
from jax.sharding import PartitionSpec as P

VMEM = pl.BlockSpec(memory_space=pltpu.VMEM)
SMEM = pl.BlockSpec(memory_space=pltpu.SMEM)
ANY = pl.BlockSpec(memory_space=pl.ANY)
F32 = jnp.float32


def weight_values(count):
    table = []
    for k in range(count):
        if k == 0:
            first, second = 0.0, -(count * count + 2) / 12.0
        else:
            sign = 1.0 - 2.0 * (k % 2)
            sine = math.sin(math.pi * k / count)
            first = 0.5 * sign * math.cos(math.pi * k / count) / sine
            second = -0.5 * sign / (sine * sine)
        table.append(first - 0.25 * second)
    return np.asarray(table, np.float32)


def weight_of(count, source, target):
    gap = lax.rem(source - target + count, count)
    value = jnp.float32(0.0)
    for k, entry in enumerate(weight_values(count)):
        value = jnp.where(gap == k, jnp.float32(entry), value)
    return value


def raw_masks(count):
    steps = [mask for mask in range(2, count, 2) if mask & (mask - 1) == 0]
    others = [mask for mask in range(2, count, 2) if mask & (mask - 1)]
    return [(steps[k], steps[(k + 1) % len(steps)]) for k in range(len(steps))] + [(mask, mask) for mask in others]


def held_masks(me):
    pairs = raw_masks(lax.axis_size("inst"))
    core = lax.rem(me, 2)
    return [0] + [a if a == b else jnp.where(core == 0, a, b) for a, b in pairs]


def table_kernel(out):
    me = lax.axis_index("inst")
    out[0, 0] = weight_of(lax.axis_size("inst"), me, me)


def prep_kernel(token, lam, outward, station, phi, inv_stiff, jac, near, wrap, packed, modes):
    nv, nx, ny, nz = lam.shape[1:]
    odd = lax.rem(lax.axis_index("space"), 2)

    def columns(j, carry):
        for minus, out in ((1 - odd, wrap), (odd, near)):
            plane = (nx - 1) * (1 - minus)
            total = jac[0, 1 + minus, 0, j, plane] * lam[0, 0, plane]
            for i in range(1, nv):
                total = total + jac[0, 1 + minus, i, j, plane] * lam[0, i, plane]
            out[pl.ds(pl.multiple_of(j * ny, ny), ny), :] = total
        return carry

    modes_k, stations = phi.shape
    full = phi[...]
    high = full.astype(jnp.bfloat16)
    rest = full - high.astype(F32)
    mid = rest.astype(jnp.bfloat16)
    low = (rest - mid.astype(F32)).astype(jnp.bfloat16)
    pieces = jnp.concatenate([low, mid, high], axis=0)
    rows = lax.broadcasted_iota(jnp.int32, (stations, nz), 0)
    share = jnp.zeros((modes_k, nz), F32)
    for x in range(nx):
        hot = (rows == station[x : x + 1, :]).astype(F32).astype(jnp.bfloat16)
        parts = jnp.dot(pieces, hot, preferred_element_type=F32)
        at_face = parts[:modes_k] + parts[modes_k : 2 * modes_k] + parts[2 * modes_k :]
        modes[x] = at_face
        face = outward[0, x : x + 1, :] * lam[0, 0, x, 0:1, :]
        for j in range(1, nv):
            face = face + outward[j, x : x + 1, :] * lam[0, j, x, 0:1, :]
        share = share + at_face * face
    lax.fori_loop(0, nv, columns, 0)
    row = lax.broadcasted_iota(jnp.int32, (modes_k, modes_k), 0)
    lane = lax.broadcasted_iota(jnp.int32, (modes_k, modes_k), 1)
    stiff = jnp.sum(jnp.where(row == lane, inv_stiff[...], 0.0), axis=1, keepdims=True)
    column = jnp.sum(share, axis=1, keepdims=True) * stiff
    tile_lane = lax.broadcasted_iota(jnp.int32, (8, nz), 1)
    tile = jnp.zeros((8, nz), F32)
    for group in range(modes_k // 8):
        tile = jnp.where(tile_lane == group, column[8 * group : 8 * group + 8], tile)
    packed[...] = tile
    near[nv * ny :, :] = tile
    wrap[nv * ny :, :] = tile


def share_kernel(*refs):
    held, out = refs[:-1], refs[-1]
    count = lax.axis_size("inst")
    me = lax.axis_index("inst")
    weights = [weight_of(count, me ^ mask, me ^ 1) for mask in held_masks(me)]

    def columns(j, carry):
        out[0, j] = sum(weight * block[0, j] for weight, block in zip(weights, held))
        return carry

    lax.fori_loop(0, out.shape[1], columns, 0)


def flux_kernel(lam, source, jac, out):
    nv, nx, ny, nz = lam.shape[1:]
    y = lax.broadcasted_iota(jnp.int32, (ny, nz), 0)
    z = lax.broadcasted_iota(jnp.int32, (ny, nz), 1)

    def product(d, j, x):
        total = jac[0, d, 0, j, x] * lam[0, 0, x]
        for i in range(1, nv):
            total = total + jac[0, d, i, j, x] * lam[0, i, x]
        return total

    def columns(j, carry):
        for x in range(nx):
            total = product(0, j, x) - source[0, j, x]
            if x > 0:
                total = total + product(1, j, x - 1)
            if x < nx - 1:
                total = total + product(2, j, x + 1)
            total = total + jnp.where(y == 0, 0.0, pltpu.roll(product(3, j, x), 1, 0))
            total = total + jnp.where(y == ny - 1, 0.0, pltpu.roll(product(4, j, x), ny - 1, 0))
            total = total + jnp.where(z == 0, 0.0, pltpu.roll(product(5, j, x), 1, 1))
            total = total + jnp.where(z == nz - 1, 0.0, pltpu.roll(product(6, j, x), nz - 1, 1))
            out[0, j, x] = total
        return carry

    lax.fori_loop(0, nv, columns, 0)


def own_kernel(partial, volume, packed, wrap, *refs):
    far, refs = (refs[0], refs[1:]) if len(refs) - 3 > len(raw_masks(lax.axis_size("inst"))) else (None, refs)
    held, (out, tile) = refs[:-2], refs[-2:]
    nv, nx, ny, nz = partial.shape[1:]
    count = lax.axis_size("inst")
    me = lax.axis_index("inst")
    weights = [weight_of(count, me ^ mask, me) for mask in held_masks(me)]
    plane = (nx - 1) * lax.rem(lax.axis_index("space"), 2)

    def columns(j, carry):
        total = sum(weight * block[0, j] for weight, block in zip(weights, held))
        out[0, j] = volume[...] * total + partial[0, j]
        out[0, j, plane] = out[0, j, plane] + wrap[pl.ds(pl.multiple_of(j * ny, ny), ny), :]
        return carry

    lax.fori_loop(0, nv, columns, 0)
    tile[...] = packed[...]
    if far is not None:
        tile[...] = packed[...] + wrap[nv * ny :, :] + far[...]


def final_kernel(partial, volume, modes, surface_in, mix, near, tile_in, out, modal):
    nv, nx, ny, nz = partial.shape[1:]
    groups = modal.shape[1] // 8
    tile = near[nv * ny :, :] + tile_in[...]
    even = lax.rem(lax.axis_index("space"), 2) == 0
    columns = [tile[:, group : group + 1] for group in range(groups)]
    line = None
    for group, column in enumerate(columns):
        row = lax.broadcasted_iota(jnp.int32, (8, 8 * groups), 0)
        lane = lax.broadcasted_iota(jnp.int32, (8, 8 * groups), 1)
        piece = jnp.sum(jnp.where(lane == row + 8 * group, column, 0.0), axis=0, keepdims=True)
        line = piece if line is None else line + piece
    modal[...] = line
    low = lax.broadcasted_iota(jnp.int32, (ny, nz), 0) == 0
    backs = []
    for x in range(nx):
        back = jnp.zeros((8, nz), F32)
        for group, column in enumerate(columns):
            back = back + modes[x, 8 * group : 8 * group + 8, :] * column
        backs.append(jnp.sum(back, axis=0, keepdims=True))

    def step(j, carry):
        inward = surface_in[j]
        border = near[pl.ds(pl.multiple_of(j * ny, ny), ny), :]
        for x in range(nx):
            value = partial[0, j, x] + volume[x] * mix[0, j, x]
            if x == 0:
                value = value + jnp.where(even, 0.0, border)
            if x == nx - 1:
                value = value + jnp.where(even, border, 0.0)
            out[0, j, x] = value + jnp.where(low, inward[x : x + 1, :] * backs[x], 0.0)
        return carry

    lax.fori_loop(0, nv, step, 0)


def body(adjoint, jacobian, volume, source, surface_out, surface_in, station, phi, inv_stiff):
    count, slabs = lax.axis_size("inst"), lax.axis_size("space")
    nv, nx, ny, nz = adjoint.shape[1:]
    modes_k = phi.shape[0]

    def swap(value, axis, mask):
        size = lax.axis_size(axis)
        return lax.ppermute(value, axis, [(i, i ^ mask) for i in range(size)])

    def fast(array):
        return pltpu.with_memory_space_constraint(array, pltpu.VMEM)

    def call(kernel, name, out_shape, flops, *operands, specs=None):
        return pl.pallas_call(
            kernel,
            out_shape=out_shape,
            in_specs=[VMEM] * len(operands) if specs is None else specs,
            out_specs=jax.tree.map(lambda shape: SMEM if name == "table" else VMEM, out_shape),
            compiler_params=pltpu.CompilerParams(vmem_limit_bytes=4 * 2**20),
            cost_estimate=pl.CostEstimate(flops=flops, bytes_accessed=0, transcendentals=0),
            name=name,
        )(*operands)

    block = pltpu.VMEM(adjoint.shape, F32)
    raws = [
        lax.ppermute(adjoint, "inst", [(i, i ^ pair[i % 2]) for i in range(count)]) for pair in raw_masks(count)
    ]
    rows = nv * ny + 8
    lam, jac = fast(adjoint), fast(jacobian)
    weights = call(table_kernel, "table", pltpu.SMEM((1, 1), F32), 2**31)
    near, wrap, packed, modes = call(
        prep_kernel,
        "prep",
        (
            pltpu.VMEM((rows, nz), F32),
            pltpu.VMEM((rows, nz), F32),
            pltpu.VMEM((8, nz), F32),
            pltpu.VMEM((nx, modes_k, nz), F32),
        ),
        0,
        weights,
        lam,
        fast(surface_out),
        fast(station),
        fast(phi),
        fast(inv_stiff.reshape(1, modes_k)),
        jac,
        specs=[SMEM] + [VMEM] * 6,
    )
    wrap_in = lax.ppermute(wrap, "space", [(i, (((i + 1) ^ 1) - 1) % slabs) for i in range(slabs)])
    near_in = swap(near, "space", 1)
    far_in = [swap(packed, "space", 2)] if slabs == 4 else []
    partial = call(flux_kernel, "flux", block, 2 * jacobian.size, lam, fast(source), jac)
    share = call(share_kernel, "share", block, 0, lam, *raws)
    mix = swap(share, "inst", 1)
    vol = fast(volume)
    partial, tile = call(
        own_kernel,
        "own",
        (block, pltpu.VMEM((8, nz), F32)),
        2**31,
        partial,
        vol,
        packed,
        wrap_in,
        *far_in,
        lam,
        *raws,
    )
    if slabs != 4:
        tile = tile + near_in[nv * ny :]
        step = 2
        while step < slabs:
            tile = tile + swap(tile, "space", step)
            step *= 2
        near_in = near_in.at[nv * ny :].set(0.0)
    residual, modal = call(
        final_kernel,
        "final",
        (jax.ShapeDtypeStruct(adjoint.shape, F32), jax.ShapeDtypeStruct((1, modes_k), F32)),
        0,
        partial,
        vol,
        modes,
        fast(surface_in),
        mix,
        near_in,
        tile,
    )
    return residual, modal


def solution(mesh):
    placed = (
        P("inst", None, "space", None, None),
        P("inst", None, None, None, "space", None, None),
        P("space", None, None),
        P("inst", None, "space", None, None),
        P(None, "space", None),
        P(None, "space", None),
        P("space", None),
        P(),
        P(),
    )
    return jax.shard_map(
        body,
        mesh=mesh,
        in_specs=placed,
        out_specs=(P("inst", None, "space", None, None), P("inst", None)),
        check_vma=False,
    )
```

```python
import functools
import math

import jax
import jax.numpy as jnp
import numpy as np
from jax import lax
from jax.experimental import pallas as pl
from jax.experimental.pallas import tpu as pltpu
from jax.sharding import PartitionSpec as P

VMEM = pl.BlockSpec(memory_space=pltpu.VMEM)
SMEM = pl.BlockSpec(memory_space=pltpu.SMEM)
ANY = pl.BlockSpec(memory_space=pl.ANY)
F32 = jnp.float32


def weight_values(count):
    table = []
    for k in range(count):
        if k == 0:
            first, second = 0.0, -(count * count + 2) / 12.0
        else:
            sign = 1.0 - 2.0 * (k % 2)
            sine = math.sin(math.pi * k / count)
            first = 0.5 * sign * math.cos(math.pi * k / count) / sine
            second = -0.5 * sign / (sine * sine)
        table.append(first - 0.25 * second)
    return np.asarray(table, np.float32)


def weight_of(count, source, target):
    gap = lax.rem(source - target + count, count)
    value = jnp.float32(0.0)
    for k, entry in enumerate(weight_values(count)):
        value = jnp.where(gap == k, jnp.float32(entry), value)
    return value


def raw_masks(count):
    steps = [mask for mask in range(2, count, 2) if mask & (mask - 1) == 0]
    others = [mask for mask in range(2, count, 2) if mask & (mask - 1)]
    first = [(steps[k] + 0, steps[(k + 1) % len(steps)] + 0) for k in range(len(steps))]
    return first + [(mask + 1, mask + 1) for mask in others]


def held_masks(me):
    pairs = raw_masks(lax.axis_size("inst"))
    core = lax.rem(me, 2)
    return [0] + [jnp.where(core == a % 2, a, b) for a, b in pairs]


def table_kernel(out):
    me = lax.axis_index("inst")
    out[0, 0] = weight_of(lax.axis_size("inst"), me, me)


def prep_kernel(token, lam, outward, station, phi, inv_stiff, jac, near, wrap, packed, modes):
    nv, nx, ny, nz = lam.shape[1:]
    odd = lax.rem(lax.axis_index("space"), 2)

    def columns(j, carry):
        for minus, out in ((1 - odd, wrap), (odd, near)):
            plane = (nx - 1) * (1 - minus)
            total = jac[0, 1 + minus, 0, j, plane] * lam[0, 0, plane]
            for i in range(1, nv):
                total = total + jac[0, 1 + minus, i, j, plane] * lam[0, i, plane]
            out[pl.ds(pl.multiple_of(j * ny, ny), ny), :] = total
        return carry

    modes_k, stations = phi.shape
    full = phi[...]
    high = full.astype(jnp.bfloat16)
    rest = full - high.astype(F32)
    mid = rest.astype(jnp.bfloat16)
    low = (rest - mid.astype(F32)).astype(jnp.bfloat16)
    pieces = jnp.concatenate([low, mid, high], axis=0)
    rows = lax.broadcasted_iota(jnp.int32, (stations, nz), 0)
    share = jnp.zeros((modes_k, nz), F32)
    for x in range(nx):
        hot = (rows == station[x : x + 1, :]).astype(F32).astype(jnp.bfloat16)
        parts = jnp.dot(pieces, hot, preferred_element_type=F32)
        at_face = parts[:modes_k] + parts[modes_k : 2 * modes_k] + parts[2 * modes_k :]
        modes[x] = at_face
        face = outward[0, x : x + 1, :] * lam[0, 0, x, 0:1, :]
        for j in range(1, nv):
            face = face + outward[j, x : x + 1, :] * lam[0, j, x, 0:1, :]
        share = share + at_face * face
    lax.fori_loop(0, nv, columns, 0)
    row = lax.broadcasted_iota(jnp.int32, (modes_k, modes_k), 0)
    lane = lax.broadcasted_iota(jnp.int32, (modes_k, modes_k), 1)
    stiff = jnp.sum(jnp.where(row == lane, inv_stiff[...], 0.0), axis=1, keepdims=True)
    column = jnp.sum(share, axis=1, keepdims=True) * stiff
    tile_lane = lax.broadcasted_iota(jnp.int32, (8, nz), 1)
    tile = jnp.zeros((8, nz), F32)
    for group in range(modes_k // 8):
        tile = jnp.where(tile_lane == group, column[8 * group : 8 * group + 8], tile)
    packed[...] = tile
    near[nv * ny :, :] = tile
    wrap[nv * ny :, :] = tile


def mix_kernel(partial, volume, *refs):
    held, (share, out) = refs[:-2], refs[-2:]
    count = lax.axis_size("inst")
    me = lax.axis_index("inst")
    masks = held_masks(me)
    there = [weight_of(count, me ^ mask, me ^ 1) for mask in masks]
    here = [weight_of(count, me ^ mask, me) for mask in masks]

    def columns(j, carry):
        share[0, j] = sum(weight * block[0, j] for weight, block in zip(there, held))
        total = sum(weight * block[0, j] for weight, block in zip(here, held))
        out[0, j] = volume[...] * total + partial[0, j]
        return carry

    lax.fori_loop(0, partial.shape[1], columns, 0)


def flux_kernel(lam, source, jac, out):
    nv, nx, ny, nz = lam.shape[1:]
    y = lax.broadcasted_iota(jnp.int32, (ny, nz), 0)
    z = lax.broadcasted_iota(jnp.int32, (ny, nz), 1)

    def product(d, j, x):
        total = jac[0, d, 0, j, x] * lam[0, 0, x]
        for i in range(1, nv):
            total = total + jac[0, d, i, j, x] * lam[0, i, x]
        return total

    def columns(j, carry):
        for x in range(nx):
            total = product(0, j, x) - source[0, j, x]
            if x > 0:
                total = total + product(1, j, x - 1)
            if x < nx - 1:
                total = total + product(2, j, x + 1)
            total = total + jnp.where(y == 0, 0.0, pltpu.roll(product(3, j, x), 1, 0))
            total = total + jnp.where(y == ny - 1, 0.0, pltpu.roll(product(4, j, x), ny - 1, 0))
            total = total + jnp.where(z == 0, 0.0, pltpu.roll(product(5, j, x), 1, 1))
            total = total + jnp.where(z == nz - 1, 0.0, pltpu.roll(product(6, j, x), nz - 1, 1))
            out[0, j, x] = total
        return carry

    lax.fori_loop(0, nv, columns, 0)


def pick_kernel(packed, first, second, out):
    lower = lax.axis_index("space") < 2
    split = out.shape[0] - 8
    out[:split, :] = jnp.where(lower, first[:split, :], second[:split, :])
    out[split:, :] = packed[...] + first[split:, :] + second[split:, :]


def final_kernel(partial, volume, modes, surface_in, mix, near, wrap, out, modal):
    nv, nx, ny, nz = partial.shape[1:]
    groups = modal.shape[1] // 8
    tile = near[nv * ny :, :] + wrap[nv * ny :, :]
    even = lax.rem(lax.axis_index("space"), 2) == 0
    columns = [tile[:, group : group + 1] for group in range(groups)]
    line = None
    for group, column in enumerate(columns):
        row = lax.broadcasted_iota(jnp.int32, (8, 8 * groups), 0)
        lane = lax.broadcasted_iota(jnp.int32, (8, 8 * groups), 1)
        piece = jnp.sum(jnp.where(lane == row + 8 * group, column, 0.0), axis=0, keepdims=True)
        line = piece if line is None else line + piece
    modal[...] = line
    low = lax.broadcasted_iota(jnp.int32, (ny, nz), 0) == 0
    backs = []
    for x in range(nx):
        back = jnp.zeros((8, nz), F32)
        for group, column in enumerate(columns):
            back = back + modes[x, 8 * group : 8 * group + 8, :] * column
        backs.append(jnp.sum(back, axis=0, keepdims=True))

    def step(j, carry):
        inward = surface_in[j]
        rows = pl.ds(pl.multiple_of(j * ny, ny), ny)
        first = jnp.where(even, wrap[rows, :], near[rows, :])
        last = jnp.where(even, near[rows, :], wrap[rows, :])
        for x in range(nx):
            value = partial[0, j, x] + volume[x] * mix[0, j, x]
            if x == 0:
                value = value + first
            if x == nx - 1:
                value = value + last
            out[0, j, x] = value + jnp.where(low, inward[x : x + 1, :] * backs[x], 0.0)
        return carry

    lax.fori_loop(0, nv, step, 0)


def body(adjoint, jacobian, volume, source, surface_out, surface_in, station, phi, inv_stiff):
    count, slabs = lax.axis_size("inst"), lax.axis_size("space")
    nv, nx, ny, nz = adjoint.shape[1:]
    modes_k = phi.shape[0]

    def swap(value, axis, mask):
        size = lax.axis_size(axis)
        return lax.ppermute(value, axis, [(i, i ^ mask) for i in range(size)])

    def fast(array):
        return pltpu.with_memory_space_constraint(array, pltpu.VMEM)

    def call(kernel, name, out_shape, flops, *operands, specs=None):
        return pl.pallas_call(
            kernel,
            out_shape=out_shape,
            in_specs=[VMEM] * len(operands) if specs is None else specs,
            out_specs=jax.tree.map(lambda shape: SMEM if name == "table" else VMEM, out_shape),
            compiler_params=pltpu.CompilerParams(vmem_limit_bytes=4 * 2**20),
            cost_estimate=pl.CostEstimate(flops=flops, bytes_accessed=0, transcendentals=0),
            name=name,
        )(*operands)

    block = pltpu.VMEM(adjoint.shape, F32)
    raws = [
        lax.ppermute(adjoint, "inst", [(i, i ^ pair[i % 2]) for i in range(count)]) for pair in raw_masks(count)
    ]
    rows = nv * ny + 8
    lam, jac = fast(adjoint), fast(jacobian)
    weights = call(table_kernel, "table", pltpu.SMEM((1, 1), F32), 2**31)
    near, wrap, packed, modes = call(
        prep_kernel,
        "prep",
        (
            pltpu.VMEM((rows, nz), F32),
            pltpu.VMEM((rows, nz), F32),
            pltpu.VMEM((8, nz), F32),
            pltpu.VMEM((nx, modes_k, nz), F32),
        ),
        0,
        weights,
        lam,
        fast(surface_out),
        fast(station),
        fast(phi),
        fast(inv_stiff.reshape(1, modes_k)),
        jac,
        specs=[SMEM] + [VMEM] * 6,
    )
    if slabs == 4:
        first = lax.ppermute(wrap, "space", [(3, 0), (2, 1), (0, 2), (1, 3)])
        second = lax.ppermute(wrap, "space", [(0, 3), (1, 2), (2, 0), (3, 1)])
        near_in = swap(near, "space", 1)
        wrap_in = call(pick_kernel, "pick", pltpu.VMEM((rows, nz), F32), 2**31, packed, first, second)
    else:
        wrap_in = lax.ppermute(wrap, "space", [(i, (((i + 1) ^ 1) - 1) % slabs) for i in range(slabs)])
        near_in = swap(near, "space", 1)
        tile = packed + near_in[nv * ny :]
        step = 2
        while step < slabs:
            tile = tile + swap(tile, "space", step)
            step *= 2
        wrap_in = wrap_in.at[nv * ny :].set(tile)
        near_in = near_in.at[nv * ny :].set(0.0)
    partial = call(flux_kernel, "flux", block, 2 * jacobian.size, lam, fast(source), jac)
    vol = fast(volume)
    share, partial = call(mix_kernel, "mix", (block, block), 0, partial, vol, lam, *raws)
    mix = swap(share, "inst", 1)
    residual, modal = call(
        final_kernel,
        "final",
        (jax.ShapeDtypeStruct(adjoint.shape, F32), jax.ShapeDtypeStruct((1, modes_k), F32)),
        0,
        partial,
        vol,
        modes,
        fast(surface_in),
        mix,
        near_in,
        wrap_in,
    )
    return residual, modal


def solution(mesh):
    placed = (
        P("inst", None, "space", None, None),
        P("inst", None, None, None, "space", None, None),
        P("space", None, None),
        P("inst", None, "space", None, None),
        P(None, "space", None),
        P(None, "space", None),
        P("space", None),
        P(),
        P(),
    )
    return jax.shard_map(
        body,
        mesh=mesh,
        in_specs=placed,
        out_specs=(P("inst", None, "space", None, None), P("inst", None)),
        check_vma=False,
    )
```

```python
import functools
import math

import jax
import jax.numpy as jnp
import numpy as np
from jax import lax
from jax.experimental import pallas as pl
from jax.experimental.pallas import tpu as pltpu
from jax.sharding import PartitionSpec as P

VMEM = pl.BlockSpec(memory_space=pltpu.VMEM)
SMEM = pl.BlockSpec(memory_space=pltpu.SMEM)
ANY = pl.BlockSpec(memory_space=pl.ANY)
F32 = jnp.float32


def weight_values(count):
    table = []
    for k in range(count):
        if k == 0:
            first, second = 0.0, -(count * count + 2) / 12.0
        else:
            sign = 1.0 - 2.0 * (k % 2)
            sine = math.sin(math.pi * k / count)
            first = 0.5 * sign * math.cos(math.pi * k / count) / sine
            second = -0.5 * sign / (sine * sine)
        table.append(first - 0.25 * second)
    return np.asarray(table, np.float32)


def weight_of(count, source, target):
    gap = lax.rem(source - target + count, count)
    value = jnp.float32(0.0)
    for k, entry in enumerate(weight_values(count)):
        value = jnp.where(gap == k, jnp.float32(entry), value)
    return value


def raw_masks(count):
    steps = [mask for mask in range(2, count, 2) if mask & (mask - 1) == 0]
    others = [mask for mask in range(2, count, 2) if mask & (mask - 1)]
    first = [(steps[k], steps[(k + 1) % len(steps)]) for k in range(len(steps))]
    return first + [(mask + 1, mask + 1) for mask in others]


def held_masks(me):
    pairs = raw_masks(lax.axis_size("inst"))
    core = lax.rem(me, 2)
    return [0] + [jnp.where(core == a % 2, a, b) for a, b in pairs]


def table_kernel(out):
    me = lax.axis_index("inst")
    out[0, 0] = weight_of(lax.axis_size("inst"), me, me)


def prep_kernel(token, lam, outward, station, phi, inv_stiff, jac, near, wrap, packed, modes):
    nv, nx, ny, nz = lam.shape[1:]
    odd = lax.rem(lax.axis_index("space"), 2)

    def columns(j, carry):
        for minus, out in ((1 - odd, wrap), (odd, near)):
            plane = (nx - 1) * (1 - minus)
            total = jac[0, 1 + minus, 0, j, plane] * lam[0, 0, plane]
            for i in range(1, nv):
                total = total + jac[0, 1 + minus, i, j, plane] * lam[0, i, plane]
            out[pl.ds(pl.multiple_of(j * ny, ny), ny), :] = total
        return carry

    modes_k, stations = phi.shape
    full = phi[...]
    high = full.astype(jnp.bfloat16)
    rest = full - high.astype(F32)
    mid = rest.astype(jnp.bfloat16)
    low = (rest - mid.astype(F32)).astype(jnp.bfloat16)
    pieces = jnp.concatenate([low, mid, high], axis=0)
    rows = lax.broadcasted_iota(jnp.int32, (stations, nz), 0)
    share = jnp.zeros((modes_k, nz), F32)
    for x in range(nx):
        hot = (rows == station[x : x + 1, :]).astype(F32).astype(jnp.bfloat16)
        parts = jnp.dot(pieces, hot, preferred_element_type=F32)
        at_face = parts[:modes_k] + parts[modes_k : 2 * modes_k] + parts[2 * modes_k :]
        modes[x] = at_face
        face = outward[0, x : x + 1, :] * lam[0, 0, x, 0:1, :]
        for j in range(1, nv):
            face = face + outward[j, x : x + 1, :] * lam[0, j, x, 0:1, :]
        share = share + at_face * face
    lax.fori_loop(0, nv, columns, 0)
    row = lax.broadcasted_iota(jnp.int32, (modes_k, modes_k), 0)
    lane = lax.broadcasted_iota(jnp.int32, (modes_k, modes_k), 1)
    stiff = jnp.sum(jnp.where(row == lane, inv_stiff[...], 0.0), axis=1, keepdims=True)
    column = jnp.sum(share, axis=1, keepdims=True) * stiff
    tile_lane = lax.broadcasted_iota(jnp.int32, (8, nz), 1)
    tile = jnp.zeros((8, nz), F32)
    for group in range(modes_k // 8):
        tile = jnp.where(tile_lane == group, column[8 * group : 8 * group + 8], tile)
    packed[...] = tile
    near[nv * ny :, :] = tile
    wrap[nv * ny :, :] = tile


def mix_of(held, target):
    count = lax.axis_size("inst")
    me = lax.axis_index("inst")
    weights = [weight_of(count, me ^ mask, me ^ target) for mask in held_masks(me)]
    return lambda j: sum(weight * block[0, j] for weight, block in zip(weights, held))


def share_kernel(after, *refs):
    held, out = refs[:-1], refs[-1]
    share = mix_of(held, 1)

    def columns(j, carry):
        out[0, j] = share(j)
        return carry

    lax.fori_loop(0, out.shape[1], columns, 0)


def flux_kernel(after, lam, source, jac, out):
    nv, nx, ny, nz = lam.shape[1:]
    y = lax.broadcasted_iota(jnp.int32, (ny, nz), 0)
    z = lax.broadcasted_iota(jnp.int32, (ny, nz), 1)

    def product(d, j, x):
        total = jac[0, d, 0, j, x] * lam[0, 0, x]
        for i in range(1, nv):
            total = total + jac[0, d, i, j, x] * lam[0, i, x]
        return total

    def columns(j, carry):
        for x in range(nx):
            total = product(0, j, x) - source[0, j, x]
            if x > 0:
                total = total + product(1, j, x - 1)
            if x < nx - 1:
                total = total + product(2, j, x + 1)
            total = total + jnp.where(y == 0, 0.0, pltpu.roll(product(3, j, x), 1, 0))
            total = total + jnp.where(y == ny - 1, 0.0, pltpu.roll(product(4, j, x), ny - 1, 0))
            total = total + jnp.where(z == 0, 0.0, pltpu.roll(product(5, j, x), 1, 1))
            total = total + jnp.where(z == nz - 1, 0.0, pltpu.roll(product(6, j, x), nz - 1, 1))
            out[0, j, x] = total
        return carry

    lax.fori_loop(0, nv, columns, 0)


def pick_kernel(packed, first, second, out):
    lower = lax.axis_index("space") < 2
    split = out.shape[0] - 8
    out[:split, :] = jnp.where(lower, first[:split, :], second[:split, :])
    out[split:, :] = packed[...] + first[split:, :] + second[split:, :]


def beam_kernel(partial, volume, modes, surface_in, near, wrap, *refs):
    held, (out, modal) = refs[:-2], refs[-2:]
    nv, nx, ny, nz = partial.shape[1:]
    groups = modal.shape[1] // 8
    own = mix_of(held, 0)
    even = lax.rem(lax.axis_index("space"), 2) == 0
    tile = near[nv * ny :, :] + wrap[nv * ny :, :]
    columns = [tile[:, group : group + 1] for group in range(groups)]
    line = None
    for group, column in enumerate(columns):
        row = lax.broadcasted_iota(jnp.int32, (8, 8 * groups), 0)
        lane = lax.broadcasted_iota(jnp.int32, (8, 8 * groups), 1)
        piece = jnp.sum(jnp.where(lane == row + 8 * group, column, 0.0), axis=0, keepdims=True)
        line = piece if line is None else line + piece
    modal[...] = line
    low = lax.broadcasted_iota(jnp.int32, (ny, nz), 0) == 0
    backs = []
    for x in range(nx):
        back = jnp.zeros((8, nz), F32)
        for group, column in enumerate(columns):
            back = back + modes[x, 8 * group : 8 * group + 8, :] * column
        backs.append(jnp.sum(back, axis=0, keepdims=True))

    def step(j, carry):
        mixed = own(j)
        inward = surface_in[j]
        rows = pl.ds(pl.multiple_of(j * ny, ny), ny)
        first = jnp.where(even, wrap[rows, :], near[rows, :])
        last = jnp.where(even, near[rows, :], wrap[rows, :])
        for x in range(nx):
            value = partial[0, j, x] + volume[x] * mixed[x]
            if x == 0:
                value = value + first
            if x == nx - 1:
                value = value + last
            out[0, j, x] = value + jnp.where(low, inward[x : x + 1, :] * backs[x], 0.0)
        return carry

    lax.fori_loop(0, nv, step, 0)


def final_kernel(partial, volume, line, mix, out, modal):
    modal[...] = line[...]

    def columns(j, carry):
        out[0, j] = partial[0, j] + volume[...] * mix[0, j]
        return carry

    lax.fori_loop(0, out.shape[1], columns, 0)


def body(adjoint, jacobian, volume, source, surface_out, surface_in, station, phi, inv_stiff):
    count, slabs = lax.axis_size("inst"), lax.axis_size("space")
    nv, nx, ny, nz = adjoint.shape[1:]
    modes_k = phi.shape[0]

    def swap(value, axis, mask):
        size = lax.axis_size(axis)
        return lax.ppermute(value, axis, [(i, i ^ mask) for i in range(size)])

    def fast(array):
        return pltpu.with_memory_space_constraint(array, pltpu.VMEM)

    def call(kernel, name, out_shape, flops, *operands, specs=None):
        return pl.pallas_call(
            kernel,
            out_shape=out_shape,
            in_specs=[VMEM] * len(operands) if specs is None else specs,
            out_specs=jax.tree.map(lambda shape: SMEM if name == "table" else VMEM, out_shape),
            compiler_params=pltpu.CompilerParams(vmem_limit_bytes=4 * 2**20),
            cost_estimate=pl.CostEstimate(flops=flops, bytes_accessed=0, transcendentals=0),
            name=name,
        )(*operands)

    block = pltpu.VMEM(adjoint.shape, F32)
    raws = [
        lax.ppermute(adjoint, "inst", [(i, i ^ pair[i % 2]) for i in range(count)]) for pair in raw_masks(count)
    ]
    rows = nv * ny + 8
    lam, jac = fast(adjoint), fast(jacobian)
    weights = call(table_kernel, "table", pltpu.SMEM((1, 1), F32), 2**31)
    near, wrap, packed, modes = call(
        prep_kernel,
        "prep",
        (
            pltpu.VMEM((rows, nz), F32),
            pltpu.VMEM((rows, nz), F32),
            pltpu.VMEM((8, nz), F32),
            pltpu.VMEM((nx, modes_k, nz), F32),
        ),
        0,
        weights,
        lam,
        fast(surface_out),
        fast(station),
        fast(phi),
        fast(inv_stiff.reshape(1, modes_k)),
        jac,
        specs=[SMEM] + [VMEM] * 6,
    )
    if slabs == 4:
        first = lax.ppermute(wrap, "space", [(3, 0), (2, 1), (0, 2), (1, 3)])
        second = lax.ppermute(wrap, "space", [(0, 3), (1, 2), (2, 0), (3, 1)])
        near_in = swap(near, "space", 1)
        wrap_in = call(pick_kernel, "pick", pltpu.VMEM((rows, nz), F32), 2**31, packed, first, second)
    else:
        wrap_in = lax.ppermute(wrap, "space", [(i, (((i + 1) ^ 1) - 1) % slabs) for i in range(slabs)])
        near_in = swap(near, "space", 1)
        tile = packed + near_in[nv * ny :]
        step = 2
        while step < slabs:
            tile = tile + swap(tile, "space", step)
            step *= 2
        wrap_in = wrap_in.at[nv * ny :].set(tile)
        near_in = near_in.at[nv * ny :].set(0.0)
    partial = call(flux_kernel, "flux", block, 2 * jacobian.size, raws[0], lam, fast(source), jac, specs=[ANY] + [VMEM] * 3)
    vol = fast(volume)
    share = call(share_kernel, "share", block, 0, partial, lam, *raws, specs=[ANY] + [VMEM] * (1 + len(raws)))
    mix = swap(share, "inst", 1)
    partial, line = call(
        beam_kernel,
        "beam",
        (block, pltpu.VMEM((1, modes_k), F32)),
        0,
        partial,
        vol,
        modes,
        fast(surface_in),
        near_in,
        wrap_in,
        lam,
        *raws,
    )
    shapes = (jax.ShapeDtypeStruct(adjoint.shape, F32), jax.ShapeDtypeStruct((1, modes_k), F32))
    residual, modal = call(final_kernel, "final", shapes, 0, partial, vol, line, mix)
    return residual, modal


def solution(mesh):
    placed = (
        P("inst", None, "space", None, None),
        P("inst", None, None, None, "space", None, None),
        P("space", None, None),
        P("inst", None, "space", None, None),
        P(None, "space", None),
        P(None, "space", None),
        P("space", None),
        P(),
        P(),
    )
    return jax.shard_map(
        body,
        mesh=mesh,
        in_specs=placed,
        out_specs=(P("inst", None, "space", None, None), P("inst", None)),
        check_vma=False,
    )
```

```python
import functools
import math

import jax
import jax.numpy as jnp
import numpy as np
from jax import lax
from jax.experimental import pallas as pl
from jax.experimental.pallas import tpu as pltpu
from jax.sharding import PartitionSpec as P

VMEM = pl.BlockSpec(memory_space=pltpu.VMEM)
SMEM = pl.BlockSpec(memory_space=pltpu.SMEM)
ANY = pl.BlockSpec(memory_space=pl.ANY)
F32 = jnp.float32


def weight_values(count):
    table = []
    for k in range(count):
        if k == 0:
            first, second = 0.0, -(count * count + 2) / 12.0
        else:
            sign = 1.0 - 2.0 * (k % 2)
            sine = math.sin(math.pi * k / count)
            first = 0.5 * sign * math.cos(math.pi * k / count) / sine
            second = -0.5 * sign / (sine * sine)
        table.append(first - 0.25 * second)
    return np.asarray(table, np.float32)


def weight_of(count, source, target):
    gap = lax.rem(source - target + count, count)
    value = jnp.float32(0.0)
    for k, entry in enumerate(weight_values(count)):
        value = jnp.where(gap == k, jnp.float32(entry), value)
    return value


def raw_masks(count):
    steps = [mask for mask in range(2, count, 2) if mask & (mask - 1) == 0]
    others = [mask for mask in range(2, count, 2) if mask & (mask - 1)]
    first = [(steps[k], steps[(k + 1) % len(steps)]) for k in range(len(steps))]
    return first + [(mask + 1, mask + 1) for mask in others]


def held_masks(me):
    pairs = raw_masks(lax.axis_size("inst"))
    core = lax.rem(me, 2)
    return [0] + [jnp.where(core == a % 2, a, b) for a, b in pairs]


def table_kernel(out):
    me = lax.axis_index("inst")
    out[0, 0] = weight_of(lax.axis_size("inst"), me, me)


def prep_kernel(token, lam, outward, station, phi, inv_stiff, jac, near, wrap, packed, modes):
    nv, nx, ny, nz = lam.shape[1:]
    odd = lax.rem(lax.axis_index("space"), 2)

    def columns(j, carry):
        for minus, out in ((1 - odd, wrap), (odd, near)):
            plane = (nx - 1) * (1 - minus)
            total = jac[0, 1 + minus, 0, j, plane] * lam[0, 0, plane]
            for i in range(1, nv):
                total = total + jac[0, 1 + minus, i, j, plane] * lam[0, i, plane]
            out[pl.ds(pl.multiple_of(j * ny, ny), ny), :] = total
        return carry

    modes_k, stations = phi.shape
    full = phi[...]
    high = full.astype(jnp.bfloat16)
    rest = full - high.astype(F32)
    mid = rest.astype(jnp.bfloat16)
    low = (rest - mid.astype(F32)).astype(jnp.bfloat16)
    pieces = jnp.concatenate([low, mid, high], axis=0)
    rows = lax.broadcasted_iota(jnp.int32, (stations, nz), 0)
    share = jnp.zeros((modes_k, nz), F32)
    for x in range(nx):
        hot = (rows == station[x : x + 1, :]).astype(F32).astype(jnp.bfloat16)
        parts = jnp.dot(pieces, hot, preferred_element_type=F32)
        at_face = parts[:modes_k] + parts[modes_k : 2 * modes_k] + parts[2 * modes_k :]
        modes[x] = at_face
        face = outward[0, x : x + 1, :] * lam[0, 0, x, 0:1, :]
        for j in range(1, nv):
            face = face + outward[j, x : x + 1, :] * lam[0, j, x, 0:1, :]
        share = share + at_face * face
    lax.fori_loop(0, nv, columns, 0)
    row = lax.broadcasted_iota(jnp.int32, (modes_k, modes_k), 0)
    lane = lax.broadcasted_iota(jnp.int32, (modes_k, modes_k), 1)
    stiff = jnp.sum(jnp.where(row == lane, inv_stiff[...], 0.0), axis=1, keepdims=True)
    column = jnp.sum(share, axis=1, keepdims=True) * stiff
    tile_lane = lax.broadcasted_iota(jnp.int32, (8, nz), 1)
    tile = jnp.zeros((8, nz), F32)
    for group in range(modes_k // 8):
        tile = jnp.where(tile_lane == group, column[8 * group : 8 * group + 8], tile)
    packed[...] = tile
    near[nv * ny :, :] = tile
    wrap[nv * ny :, :] = tile


def mix_of(held, target, skip=0, core=0):
    count = lax.axis_size("inst")
    me = lax.axis_index("inst")
    there = me ^ core
    weights = [weight_of(count, there ^ mask, me ^ target) for mask in held_masks(there)[skip:]]
    return lambda j: sum(weight * block[0, j] for weight, block in zip(weights, held))


def share_kernel(after, *refs):
    held, out = refs[:-1], refs[-1]
    share = mix_of(held, 1)

    def columns(j, carry):
        out[0, j] = share(j)
        return carry

    lax.fori_loop(0, out.shape[1], columns, 0)


def flux_kernel(after, lam, source, jac, out):
    nv, nx, ny, nz = lam.shape[1:]
    y = lax.broadcasted_iota(jnp.int32, (ny, nz), 0)
    z = lax.broadcasted_iota(jnp.int32, (ny, nz), 1)

    def product(d, j, x):
        total = jac[0, d, 0, j, x] * lam[0, 0, x]
        for i in range(1, nv):
            total = total + jac[0, d, i, j, x] * lam[0, i, x]
        return total

    def columns(j, carry):
        for x in range(nx):
            total = product(0, j, x) - source[0, j, x]
            if x > 0:
                total = total + product(1, j, x - 1)
            if x < nx - 1:
                total = total + product(2, j, x + 1)
            total = total + jnp.where(y == 0, 0.0, pltpu.roll(product(3, j, x), 1, 0))
            total = total + jnp.where(y == ny - 1, 0.0, pltpu.roll(product(4, j, x), ny - 1, 0))
            total = total + jnp.where(z == 0, 0.0, pltpu.roll(product(5, j, x), 1, 1))
            total = total + jnp.where(z == nz - 1, 0.0, pltpu.roll(product(6, j, x), nz - 1, 1))
            out[0, j, x] = total
        return carry

    lax.fori_loop(0, nv, columns, 0)


def pick_kernel(packed, first, second, out):
    lower = lax.axis_index("space") < 2
    split = out.shape[0] - 8
    out[:split, :] = jnp.where(lower, first[:split, :], second[:split, :])
    out[split:, :] = packed[...] + first[split:, :] + second[split:, :]


def beam_kernel(partial, volume, modes, surface_in, near, wrap, *refs):
    held, (out, modal) = refs[:-2], refs[-2:]
    nv, nx, ny, nz = partial.shape[1:]
    groups = modal.shape[1] // 8
    own = mix_of(held, 0)
    even = lax.rem(lax.axis_index("space"), 2) == 0
    tile = near[nv * ny :, :] + wrap[nv * ny :, :]
    columns = [tile[:, group : group + 1] for group in range(groups)]
    line = None
    for group, column in enumerate(columns):
        row = lax.broadcasted_iota(jnp.int32, (8, 8 * groups), 0)
        lane = lax.broadcasted_iota(jnp.int32, (8, 8 * groups), 1)
        piece = jnp.sum(jnp.where(lane == row + 8 * group, column, 0.0), axis=0, keepdims=True)
        line = piece if line is None else line + piece
    modal[...] = line
    low = lax.broadcasted_iota(jnp.int32, (ny, nz), 0) == 0
    backs = []
    for x in range(nx):
        back = jnp.zeros((8, nz), F32)
        for group, column in enumerate(columns):
            back = back + modes[x, 8 * group : 8 * group + 8, :] * column
        backs.append(jnp.sum(back, axis=0, keepdims=True))

    def step(j, carry):
        mixed = own(j)
        inward = surface_in[j]
        rows = pl.ds(pl.multiple_of(j * ny, ny), ny)
        first = jnp.where(even, wrap[rows, :], near[rows, :])
        last = jnp.where(even, near[rows, :], wrap[rows, :])
        for x in range(nx):
            value = partial[0, j, x] + volume[x] * mixed[x]
            if x == 0:
                value = value + first
            if x == nx - 1:
                value = value + last
            out[0, j, x] = value + jnp.where(low, inward[x : x + 1, :] * backs[x], 0.0)
        return carry

    lax.fori_loop(0, nv, step, 0)


def final_kernel(partial, volume, line, mix, *refs):
    last, (out, modal) = refs[:-2], refs[-2:]
    modal[...] = line[...]
    rest = mix_of(last, 0, len(held_masks(0)) - len(last), 1)

    def columns(j, carry):
        out[0, j] = partial[0, j] + volume[...] * (mix[0, j] + rest(j))
        return carry

    lax.fori_loop(0, out.shape[1], columns, 0)


def body(adjoint, jacobian, volume, source, surface_out, surface_in, station, phi, inv_stiff):
    count, slabs = lax.axis_size("inst"), lax.axis_size("space")
    nv, nx, ny, nz = adjoint.shape[1:]
    modes_k = phi.shape[0]

    def swap(value, axis, mask):
        size = lax.axis_size(axis)
        return lax.ppermute(value, axis, [(i, i ^ mask) for i in range(size)])

    def fast(array):
        return pltpu.with_memory_space_constraint(array, pltpu.VMEM)

    def call(kernel, name, out_shape, flops, *operands, specs=None):
        return pl.pallas_call(
            kernel,
            out_shape=out_shape,
            in_specs=[VMEM] * len(operands) if specs is None else specs,
            out_specs=jax.tree.map(lambda shape: SMEM if name == "table" else VMEM, out_shape),
            compiler_params=pltpu.CompilerParams(vmem_limit_bytes=4 * 2**20),
            cost_estimate=pl.CostEstimate(flops=flops, bytes_accessed=0, transcendentals=0),
            name=name,
        )(*operands)

    block = pltpu.VMEM(adjoint.shape, F32)
    raws = [
        lax.ppermute(adjoint, "inst", [(i, i ^ pair[i % 2]) for i in range(count)]) for pair in raw_masks(count)
    ]
    steps = sum(mask & (mask - 1) == 0 for mask in range(2, count, 2))
    rows = nv * ny + 8
    lam, jac = fast(adjoint), fast(jacobian)
    weights = call(table_kernel, "table", pltpu.SMEM((1, 1), F32), 2**31)
    near, wrap, packed, modes = call(
        prep_kernel,
        "prep",
        (
            pltpu.VMEM((rows, nz), F32),
            pltpu.VMEM((rows, nz), F32),
            pltpu.VMEM((8, nz), F32),
            pltpu.VMEM((nx, modes_k, nz), F32),
        ),
        0,
        weights,
        lam,
        fast(surface_out),
        fast(station),
        fast(phi),
        fast(inv_stiff.reshape(1, modes_k)),
        jac,
        specs=[SMEM] + [VMEM] * 6,
    )
    if slabs == 4:
        first = lax.ppermute(wrap, "space", [(3, 0), (2, 1), (0, 2), (1, 3)])
        second = lax.ppermute(wrap, "space", [(0, 3), (1, 2), (2, 0), (3, 1)])
        near_in = swap(near, "space", 1)
        wrap_in = call(pick_kernel, "pick", pltpu.VMEM((rows, nz), F32), 2**31, packed, first, second)
    else:
        wrap_in = lax.ppermute(wrap, "space", [(i, (((i + 1) ^ 1) - 1) % slabs) for i in range(slabs)])
        near_in = swap(near, "space", 1)
        tile = packed + near_in[nv * ny :]
        step = 2
        while step < slabs:
            tile = tile + swap(tile, "space", step)
            step *= 2
        wrap_in = wrap_in.at[nv * ny :].set(tile)
        near_in = near_in.at[nv * ny :].set(0.0)
    partial = call(flux_kernel, "flux", block, 2 * jacobian.size, raws[0], lam, fast(source), jac, specs=[ANY] + [VMEM] * 3)
    vol = fast(volume)
    share = call(share_kernel, "share", block, 0, partial, lam, *raws[:steps], specs=[ANY] + [VMEM] * (1 + steps))
    mix = swap(share, "inst", 1)
    last = [swap(block, "inst", 1) for block in raws[steps:]]
    partial, line = call(
        beam_kernel,
        "beam",
        (block, pltpu.VMEM((1, modes_k), F32)),
        0,
        partial,
        vol,
        modes,
        fast(surface_in),
        near_in,
        wrap_in,
        lam,
        *raws,
    )
    shapes = (jax.ShapeDtypeStruct(adjoint.shape, F32), jax.ShapeDtypeStruct((1, modes_k), F32))
    residual, modal = call(final_kernel, "final", shapes, 0, partial, vol, line, mix, *last)
    return residual, modal


def solution(mesh):
    placed = (
        P("inst", None, "space", None, None),
        P("inst", None, None, None, "space", None, None),
        P("space", None, None),
        P("inst", None, "space", None, None),
        P(None, "space", None),
        P(None, "space", None),
        P("space", None),
        P(),
        P(),
    )
    return jax.shard_map(
        body,
        mesh=mesh,
        in_specs=placed,
        out_specs=(P("inst", None, "space", None, None), P("inst", None)),
        check_vma=False,
    )
```

```python
import functools
import math

import jax
import jax.numpy as jnp
import numpy as np
from jax import lax
from jax.experimental import pallas as pl
from jax.experimental.pallas import tpu as pltpu
from jax.sharding import PartitionSpec as P

VMEM = pl.BlockSpec(memory_space=pltpu.VMEM)
SMEM = pl.BlockSpec(memory_space=pltpu.SMEM)
ANY = pl.BlockSpec(memory_space=pl.ANY)
F32 = jnp.float32


def weight_values(count):
    table = []
    for k in range(count):
        if k == 0:
            first, second = 0.0, -(count * count + 2) / 12.0
        else:
            sign = 1.0 - 2.0 * (k % 2)
            sine = math.sin(math.pi * k / count)
            first = 0.5 * sign * math.cos(math.pi * k / count) / sine
            second = -0.5 * sign / (sine * sine)
        table.append(first - 0.25 * second)
    return np.asarray(table, np.float32)


def weight_of(count, source, target):
    gap = lax.rem(source - target + count, count)
    value = jnp.float32(0.0)
    for k, entry in enumerate(weight_values(count)):
        value = jnp.where(gap == k, jnp.float32(entry), value)
    return value


def raw_masks(count):
    steps = [mask for mask in range(2, count, 2) if mask & (mask - 1) == 0]
    others = [mask for mask in range(2, count, 2) if mask & (mask - 1)]
    first = [(steps[k], steps[(k + 1) % len(steps)]) for k in range(len(steps))]
    return first + [(mask + 1, mask + 1) for mask in others]


def held_masks(me):
    pairs = raw_masks(lax.axis_size("inst"))
    core = lax.rem(me, 2)
    return [0] + [jnp.where(core == a % 2, a, b) for a, b in pairs]


def table_kernel(out):
    me = lax.axis_index("inst")
    out[0, 0] = weight_of(lax.axis_size("inst"), me, me)


def prep_kernel(token, lam, outward, station, phi, inv_stiff, jac, near, wrap, packed, modes):
    nv, nx, ny, nz = lam.shape[1:]
    odd = lax.rem(lax.axis_index("space"), 2)

    def columns(j, carry):
        for minus, out in ((1 - odd, wrap), (odd, near)):
            plane = (nx - 1) * (1 - minus)
            total = jac[0, 1 + minus, 0, j, plane] * lam[0, 0, plane]
            for i in range(1, nv):
                total = total + jac[0, 1 + minus, i, j, plane] * lam[0, i, plane]
            out[pl.ds(pl.multiple_of(j * ny, ny), ny), :] = total
        return carry

    modes_k, stations = phi.shape
    full = phi[...]
    high = full.astype(jnp.bfloat16)
    rest = full - high.astype(F32)
    mid = rest.astype(jnp.bfloat16)
    low = (rest - mid.astype(F32)).astype(jnp.bfloat16)
    pieces = jnp.concatenate([low, mid, high], axis=0)
    rows = lax.broadcasted_iota(jnp.int32, (stations, nz), 0)
    share = jnp.zeros((modes_k, nz), F32)
    for x in range(nx):
        hot = (rows == station[x : x + 1, :]).astype(F32).astype(jnp.bfloat16)
        parts = jnp.dot(pieces, hot, preferred_element_type=F32)
        at_face = parts[:modes_k] + parts[modes_k : 2 * modes_k] + parts[2 * modes_k :]
        modes[x] = at_face
        face = outward[0, x : x + 1, :] * lam[0, 0, x, 0:1, :]
        for j in range(1, nv):
            face = face + outward[j, x : x + 1, :] * lam[0, j, x, 0:1, :]
        share = share + at_face * face
    lax.fori_loop(0, nv, columns, 0)
    row = lax.broadcasted_iota(jnp.int32, (modes_k, modes_k), 0)
    lane = lax.broadcasted_iota(jnp.int32, (modes_k, modes_k), 1)
    stiff = jnp.sum(jnp.where(row == lane, inv_stiff[...], 0.0), axis=1, keepdims=True)
    column = jnp.sum(share, axis=1, keepdims=True) * stiff
    tile_lane = lax.broadcasted_iota(jnp.int32, (8, nz), 1)
    tile = jnp.zeros((8, nz), F32)
    for group in range(modes_k // 8):
        tile = jnp.where(tile_lane == group, column[8 * group : 8 * group + 8], tile)
    packed[...] = tile
    near[nv * ny :, :] = tile
    wrap[nv * ny :, :] = tile


def mix_of(held, target, skip=0, core=0):
    count = lax.axis_size("inst")
    me = lax.axis_index("inst")
    there = me ^ core
    weights = [weight_of(count, there ^ mask, me ^ target) for mask in held_masks(there)[skip:]]
    return lambda j: sum(weight * block[0, j] for weight, block in zip(weights, held))


def share_kernel(partial, volume, *refs):
    held, (out, own) = refs[:-2], refs[-2:]
    there, here = mix_of(held, 1), mix_of(held, 0)

    def columns(j, carry):
        out[0, j] = there(j)
        own[0, j] = volume[...] * here(j) + partial[0, j]
        return carry

    lax.fori_loop(0, out.shape[1], columns, 0)


def flux_kernel(after, lam, source, jac, out):
    nv, nx, ny, nz = lam.shape[1:]
    y = lax.broadcasted_iota(jnp.int32, (ny, nz), 0)
    z = lax.broadcasted_iota(jnp.int32, (ny, nz), 1)

    def product(d, j, x):
        total = jac[0, d, 0, j, x] * lam[0, 0, x]
        for i in range(1, nv):
            total = total + jac[0, d, i, j, x] * lam[0, i, x]
        return total

    def columns(j, carry):
        for x in range(nx):
            total = product(0, j, x) - source[0, j, x]
            if x > 0:
                total = total + product(1, j, x - 1)
            if x < nx - 1:
                total = total + product(2, j, x + 1)
            total = total + jnp.where(y == 0, 0.0, pltpu.roll(product(3, j, x), 1, 0))
            total = total + jnp.where(y == ny - 1, 0.0, pltpu.roll(product(4, j, x), ny - 1, 0))
            total = total + jnp.where(z == 0, 0.0, pltpu.roll(product(5, j, x), 1, 1))
            total = total + jnp.where(z == nz - 1, 0.0, pltpu.roll(product(6, j, x), nz - 1, 1))
            out[0, j, x] = total
        return carry

    lax.fori_loop(0, nv, columns, 0)


def pick_kernel(packed, first, second, out):
    lower = lax.axis_index("space") < 2
    split = out.shape[0] - 8
    out[:split, :] = jnp.where(lower, first[:split, :], second[:split, :])
    out[split:, :] = packed[...] + first[split:, :] + second[split:, :]


def beam_kernel(partial, volume, modes, surface_in, near, wrap, *refs):
    held, (out, modal) = refs[:-2], refs[-2:]
    nv, nx, ny, nz = partial.shape[1:]
    groups = modal.shape[1] // 8
    own = mix_of(held, 0, len(held_masks(0)) - len(held))
    even = lax.rem(lax.axis_index("space"), 2) == 0
    tile = near[nv * ny :, :] + wrap[nv * ny :, :]
    columns = [tile[:, group : group + 1] for group in range(groups)]
    line = None
    for group, column in enumerate(columns):
        row = lax.broadcasted_iota(jnp.int32, (8, 8 * groups), 0)
        lane = lax.broadcasted_iota(jnp.int32, (8, 8 * groups), 1)
        piece = jnp.sum(jnp.where(lane == row + 8 * group, column, 0.0), axis=0, keepdims=True)
        line = piece if line is None else line + piece
    modal[...] = line
    low = lax.broadcasted_iota(jnp.int32, (ny, nz), 0) == 0
    backs = []
    for x in range(nx):
        back = jnp.zeros((8, nz), F32)
        for group, column in enumerate(columns):
            back = back + modes[x, 8 * group : 8 * group + 8, :] * column
        backs.append(jnp.sum(back, axis=0, keepdims=True))

    def step(j, carry):
        mixed = own(j)
        inward = surface_in[j]
        rows = pl.ds(pl.multiple_of(j * ny, ny), ny)
        first = jnp.where(even, wrap[rows, :], near[rows, :])
        last = jnp.where(even, near[rows, :], wrap[rows, :])
        for x in range(nx):
            value = partial[0, j, x] + volume[x] * mixed[x]
            if x == 0:
                value = value + first
            if x == nx - 1:
                value = value + last
            out[0, j, x] = value + jnp.where(low, inward[x : x + 1, :] * backs[x], 0.0)
        return carry

    lax.fori_loop(0, nv, step, 0)


def final_kernel(partial, volume, line, mix, *refs):
    last, (out, modal) = refs[:-2], refs[-2:]
    modal[...] = line[...]
    rest = mix_of(last, 0, len(held_masks(0)) - len(last), 1)

    def columns(j, carry):
        out[0, j] = partial[0, j] + volume[...] * (mix[0, j] + rest(j))
        return carry

    lax.fori_loop(0, out.shape[1], columns, 0)


def body(adjoint, jacobian, volume, source, surface_out, surface_in, station, phi, inv_stiff):
    count, slabs = lax.axis_size("inst"), lax.axis_size("space")
    nv, nx, ny, nz = adjoint.shape[1:]
    modes_k = phi.shape[0]

    def swap(value, axis, mask):
        size = lax.axis_size(axis)
        return lax.ppermute(value, axis, [(i, i ^ mask) for i in range(size)])

    def fast(array):
        return pltpu.with_memory_space_constraint(array, pltpu.VMEM)

    def call(kernel, name, out_shape, flops, *operands, specs=None):
        return pl.pallas_call(
            kernel,
            out_shape=out_shape,
            in_specs=[VMEM] * len(operands) if specs is None else specs,
            out_specs=jax.tree.map(lambda shape: SMEM if name == "table" else VMEM, out_shape),
            compiler_params=pltpu.CompilerParams(vmem_limit_bytes=4 * 2**20),
            cost_estimate=pl.CostEstimate(flops=flops, bytes_accessed=0, transcendentals=0),
            name=name,
        )(*operands)

    block = pltpu.VMEM(adjoint.shape, F32)
    raws = [
        lax.ppermute(adjoint, "inst", [(i, i ^ pair[i % 2]) for i in range(count)]) for pair in raw_masks(count)
    ]
    steps = sum(mask & (mask - 1) == 0 for mask in range(2, count, 2))
    rows = nv * ny + 8
    lam, jac = fast(adjoint), fast(jacobian)
    weights = call(table_kernel, "table", pltpu.SMEM((1, 1), F32), 2**33)
    near, wrap, packed, modes = call(
        prep_kernel,
        "prep",
        (
            pltpu.VMEM((rows, nz), F32),
            pltpu.VMEM((rows, nz), F32),
            pltpu.VMEM((8, nz), F32),
            pltpu.VMEM((nx, modes_k, nz), F32),
        ),
        0,
        weights,
        lam,
        fast(surface_out),
        fast(station),
        fast(phi),
        fast(inv_stiff.reshape(1, modes_k)),
        jac,
        specs=[SMEM] + [VMEM] * 6,
    )
    if slabs == 4:
        first = lax.ppermute(wrap, "space", [(3, 0), (2, 1), (0, 2), (1, 3)])
        second = lax.ppermute(wrap, "space", [(0, 3), (1, 2), (2, 0), (3, 1)])
        near_in = swap(near, "space", 1)
        wrap_in = call(pick_kernel, "pick", pltpu.VMEM((rows, nz), F32), 2**31, packed, first, second)
    else:
        wrap_in = lax.ppermute(wrap, "space", [(i, (((i + 1) ^ 1) - 1) % slabs) for i in range(slabs)])
        near_in = swap(near, "space", 1)
        tile = packed + near_in[nv * ny :]
        step = 2
        while step < slabs:
            tile = tile + swap(tile, "space", step)
            step *= 2
        wrap_in = wrap_in.at[nv * ny :].set(tile)
        near_in = near_in.at[nv * ny :].set(0.0)
    partial = call(flux_kernel, "flux", block, 2 * jacobian.size, raws[0], lam, fast(source), jac, specs=[ANY] + [VMEM] * 3)
    vol = fast(volume)
    share, partial = call(share_kernel, "share", (block, block), 0, partial, vol, lam, *raws[:steps])
    mix = swap(share, "inst", 1)
    last = [swap(block, "inst", 1) for block in raws[steps:]]
    partial, line = call(
        beam_kernel,
        "beam",
        (block, pltpu.VMEM((1, modes_k), F32)),
        0,
        partial,
        vol,
        modes,
        fast(surface_in),
        near_in,
        wrap_in,
        *raws[steps:],
    )
    shapes = (jax.ShapeDtypeStruct(adjoint.shape, F32), jax.ShapeDtypeStruct((1, modes_k), F32))
    residual, modal = call(final_kernel, "final", shapes, 0, partial, vol, line, mix, *last)
    return residual, modal


def solution(mesh):
    placed = (
        P("inst", None, "space", None, None),
        P("inst", None, None, None, "space", None, None),
        P("space", None, None),
        P("inst", None, "space", None, None),
        P(None, "space", None),
        P(None, "space", None),
        P("space", None),
        P(),
        P(),
    )
    return jax.shard_map(
        body,
        mesh=mesh,
        in_specs=placed,
        out_specs=(P("inst", None, "space", None, None), P("inst", None)),
        check_vma=False,
    )
```

```python
import functools
import math

import jax
import jax.numpy as jnp
import numpy as np
from jax import lax
from jax.experimental import pallas as pl
from jax.experimental.pallas import tpu as pltpu
from jax.sharding import PartitionSpec as P

VMEM = pl.BlockSpec(memory_space=pltpu.VMEM)
SMEM = pl.BlockSpec(memory_space=pltpu.SMEM)
ANY = pl.BlockSpec(memory_space=pl.ANY)
F32 = jnp.float32


def weight_values(count):
    table = []
    for k in range(count):
        if k == 0:
            first, second = 0.0, -(count * count + 2) / 12.0
        else:
            sign = 1.0 - 2.0 * (k % 2)
            sine = math.sin(math.pi * k / count)
            first = 0.5 * sign * math.cos(math.pi * k / count) / sine
            second = -0.5 * sign / (sine * sine)
        table.append(first - 0.25 * second)
    return np.asarray(table, np.float32)


def weight_of(count, source, target):
    gap = lax.rem(source - target + count, count)
    value = jnp.float32(0.0)
    for k, entry in enumerate(weight_values(count)):
        value = jnp.where(gap == k, jnp.float32(entry), value)
    return value


def raw_masks(count):
    steps = [mask for mask in range(2, count, 2) if mask & (mask - 1) == 0]
    others = [mask for mask in range(2, count, 2) if mask & (mask - 1)]
    first = [(steps[k], steps[(k + 1) % len(steps)]) for k in range(len(steps))]
    return first + [(mask + 1, mask + 1) for mask in others]


def held_masks(me):
    pairs = raw_masks(lax.axis_size("inst"))
    core = lax.rem(me, 2)
    return [0] + [jnp.where(core == a % 2, a, b) for a, b in pairs]


def table_kernel(out):
    me = lax.axis_index("inst")
    out[0, 0] = weight_of(lax.axis_size("inst"), me, me)


def hold_kernel(token, lam, out):
    out[...] = lam[...]


def prep_kernel(token, lam, outward, station, phi, inv_stiff, jac, near, wrap, packed, modes):
    nv, nx, ny, nz = lam.shape[1:]
    odd = lax.rem(lax.axis_index("space"), 2)

    def columns(j, carry):
        for minus, out in ((1 - odd, wrap), (odd, near)):
            plane = (nx - 1) * (1 - minus)
            total = jac[0, 1 + minus, 0, j, plane] * lam[0, 0, plane]
            for i in range(1, nv):
                total = total + jac[0, 1 + minus, i, j, plane] * lam[0, i, plane]
            out[pl.ds(pl.multiple_of(j * ny, ny), ny), :] = total
        return carry

    modes_k, stations = phi.shape
    full = phi[...]
    high = full.astype(jnp.bfloat16)
    rest = full - high.astype(F32)
    mid = rest.astype(jnp.bfloat16)
    low = (rest - mid.astype(F32)).astype(jnp.bfloat16)
    pieces = jnp.concatenate([low, mid, high], axis=0)
    rows = lax.broadcasted_iota(jnp.int32, (stations, nz), 0)
    share = jnp.zeros((modes_k, nz), F32)
    for x in range(nx):
        hot = (rows == station[x : x + 1, :]).astype(F32).astype(jnp.bfloat16)
        parts = jnp.dot(pieces, hot, preferred_element_type=F32)
        at_face = parts[:modes_k] + parts[modes_k : 2 * modes_k] + parts[2 * modes_k :]
        modes[x] = at_face
        face = outward[0, x : x + 1, :] * lam[0, 0, x, 0:1, :]
        for j in range(1, nv):
            face = face + outward[j, x : x + 1, :] * lam[0, j, x, 0:1, :]
        share = share + at_face * face
    lax.fori_loop(0, nv, columns, 0)
    row = lax.broadcasted_iota(jnp.int32, (modes_k, modes_k), 0)
    lane = lax.broadcasted_iota(jnp.int32, (modes_k, modes_k), 1)
    stiff = jnp.sum(jnp.where(row == lane, inv_stiff[...], 0.0), axis=1, keepdims=True)
    column = jnp.sum(share, axis=1, keepdims=True) * stiff
    tile_lane = lax.broadcasted_iota(jnp.int32, (8, nz), 1)
    tile = jnp.zeros((8, nz), F32)
    for group in range(modes_k // 8):
        tile = jnp.where(tile_lane == group, column[8 * group : 8 * group + 8], tile)
    packed[...] = tile
    near[nv * ny :, :] = tile
    wrap[nv * ny :, :] = tile


def mix_of(held, target, skip=0, core=0):
    count = lax.axis_size("inst")
    me = lax.axis_index("inst")
    there = me ^ core
    weights = [weight_of(count, there ^ mask, me ^ target) for mask in held_masks(there)[skip:]]
    return lambda j: sum(weight * block[0, j] for weight, block in zip(weights, held))


def share_kernel(partial, volume, *refs):
    held, (out, own) = refs[:-2], refs[-2:]
    there, here = mix_of(held, 1), mix_of(held, 0)

    def columns(j, carry):
        out[0, j] = there(j)
        own[0, j] = volume[...] * here(j) + partial[0, j]
        return carry

    lax.fori_loop(0, out.shape[1], columns, 0)


def flux_kernel(after, lam, source, jac, out):
    nv, nx, ny, nz = lam.shape[1:]
    y = lax.broadcasted_iota(jnp.int32, (ny, nz), 0)
    z = lax.broadcasted_iota(jnp.int32, (ny, nz), 1)

    def product(d, j, x):
        total = jac[0, d, 0, j, x] * lam[0, 0, x]
        for i in range(1, nv):
            total = total + jac[0, d, i, j, x] * lam[0, i, x]
        return total

    def columns(j, carry):
        for x in range(nx):
            total = product(0, j, x) - source[0, j, x]
            if x > 0:
                total = total + product(1, j, x - 1)
            if x < nx - 1:
                total = total + product(2, j, x + 1)
            total = total + jnp.where(y == 0, 0.0, pltpu.roll(product(3, j, x), 1, 0))
            total = total + jnp.where(y == ny - 1, 0.0, pltpu.roll(product(4, j, x), ny - 1, 0))
            total = total + jnp.where(z == 0, 0.0, pltpu.roll(product(5, j, x), 1, 1))
            total = total + jnp.where(z == nz - 1, 0.0, pltpu.roll(product(6, j, x), nz - 1, 1))
            out[0, j, x] = total
        return carry

    lax.fori_loop(0, nv, columns, 0)


def pick_kernel(packed, first, second, out):
    lower = lax.axis_index("space") < 2
    split = out.shape[0] - 8
    out[:split, :] = jnp.where(lower, first[:split, :], second[:split, :])
    out[split:, :] = packed[...] + first[split:, :] + second[split:, :]


def beam_kernel(partial, volume, modes, surface_in, near, wrap, *refs):
    held, (out, modal) = refs[:-2], refs[-2:]
    nv, nx, ny, nz = partial.shape[1:]
    groups = modal.shape[1] // 8
    own = mix_of(held, 0, len(held_masks(0)) - len(held))
    even = lax.rem(lax.axis_index("space"), 2) == 0
    tile = near[nv * ny :, :] + wrap[nv * ny :, :]
    columns = [tile[:, group : group + 1] for group in range(groups)]
    line = None
    for group, column in enumerate(columns):
        row = lax.broadcasted_iota(jnp.int32, (8, 8 * groups), 0)
        lane = lax.broadcasted_iota(jnp.int32, (8, 8 * groups), 1)
        piece = jnp.sum(jnp.where(lane == row + 8 * group, column, 0.0), axis=0, keepdims=True)
        line = piece if line is None else line + piece
    modal[...] = line
    low = lax.broadcasted_iota(jnp.int32, (ny, nz), 0) == 0
    backs = []
    for x in range(nx):
        back = jnp.zeros((8, nz), F32)
        for group, column in enumerate(columns):
            back = back + modes[x, 8 * group : 8 * group + 8, :] * column
        backs.append(jnp.sum(back, axis=0, keepdims=True))

    def step(j, carry):
        mixed = own(j)
        inward = surface_in[j]
        rows = pl.ds(pl.multiple_of(j * ny, ny), ny)
        first = jnp.where(even, wrap[rows, :], near[rows, :])
        last = jnp.where(even, near[rows, :], wrap[rows, :])
        for x in range(nx):
            value = partial[0, j, x] + volume[x] * mixed[x]
            if x == 0:
                value = value + first
            if x == nx - 1:
                value = value + last
            out[0, j, x] = value + jnp.where(low, inward[x : x + 1, :] * backs[x], 0.0)
        return carry

    lax.fori_loop(0, nv, step, 0)


def final_kernel(partial, volume, line, mix, *refs):
    last, (out, modal) = refs[:-2], refs[-2:]
    modal[...] = line[...]
    rest = mix_of(last, 0, len(held_masks(0)) - len(last), 1)

    def columns(j, carry):
        out[0, j] = partial[0, j] + volume[...] * (mix[0, j] + rest(j))
        return carry

    lax.fori_loop(0, out.shape[1], columns, 0)


def body(adjoint, jacobian, volume, source, surface_out, surface_in, station, phi, inv_stiff):
    count, slabs = lax.axis_size("inst"), lax.axis_size("space")
    nv, nx, ny, nz = adjoint.shape[1:]
    modes_k = phi.shape[0]

    def swap(value, axis, mask):
        size = lax.axis_size(axis)
        return lax.ppermute(value, axis, [(i, i ^ mask) for i in range(size)])

    def fast(array):
        return pltpu.with_memory_space_constraint(array, pltpu.VMEM)

    def call(kernel, name, out_shape, flops, *operands, specs=None):
        return pl.pallas_call(
            kernel,
            out_shape=out_shape,
            in_specs=[VMEM] * len(operands) if specs is None else specs,
            out_specs=jax.tree.map(lambda shape: SMEM if name == "table" else VMEM, out_shape),
            compiler_params=pltpu.CompilerParams(vmem_limit_bytes=4 * 2**20),
            cost_estimate=pl.CostEstimate(flops=flops, bytes_accessed=0, transcendentals=0),
            name=name,
        )(*operands)

    block = pltpu.VMEM(adjoint.shape, F32)
    steps = sum(mask & (mask - 1) == 0 for mask in range(2, count, 2))
    lam, jac = fast(adjoint), fast(jacobian)
    weights = call(table_kernel, "table", pltpu.SMEM((1, 1), F32), 2**33)
    held = call(hold_kernel, "hold", block, 0, weights, lam, specs=[SMEM, VMEM])
    raws = [
        lax.ppermute(adjoint if k < steps else held, "inst", [(i, i ^ pair[i % 2]) for i in range(count)])
        for k, pair in enumerate(raw_masks(count))
    ]
    rows = nv * ny + 8
    near, wrap, packed, modes = call(
        prep_kernel,
        "prep",
        (
            pltpu.VMEM((rows, nz), F32),
            pltpu.VMEM((rows, nz), F32),
            pltpu.VMEM((8, nz), F32),
            pltpu.VMEM((nx, modes_k, nz), F32),
        ),
        0,
        weights,
        lam,
        fast(surface_out),
        fast(station),
        fast(phi),
        fast(inv_stiff.reshape(1, modes_k)),
        jac,
        specs=[SMEM] + [VMEM] * 6,
    )
    if slabs == 4:
        first = lax.ppermute(wrap, "space", [(3, 0), (2, 1), (0, 2), (1, 3)])
        second = lax.ppermute(wrap, "space", [(0, 3), (1, 2), (2, 0), (3, 1)])
        near_in = swap(near, "space", 1)
        wrap_in = call(pick_kernel, "pick", pltpu.VMEM((rows, nz), F32), 2**31, packed, first, second)
    else:
        wrap_in = lax.ppermute(wrap, "space", [(i, (((i + 1) ^ 1) - 1) % slabs) for i in range(slabs)])
        near_in = swap(near, "space", 1)
        tile = packed + near_in[nv * ny :]
        step = 2
        while step < slabs:
            tile = tile + swap(tile, "space", step)
            step *= 2
        wrap_in = wrap_in.at[nv * ny :].set(tile)
        near_in = near_in.at[nv * ny :].set(0.0)
    partial = call(flux_kernel, "flux", block, 2 * jacobian.size, raws[0], lam, fast(source), jac, specs=[ANY] + [VMEM] * 3)
    vol = fast(volume)
    share, partial = call(share_kernel, "share", (block, block), 0, partial, vol, lam, *raws[:steps])
    mix = swap(share, "inst", 1)
    last = [swap(block, "inst", 1) for block in raws[steps:]]
    partial, line = call(
        beam_kernel,
        "beam",
        (block, pltpu.VMEM((1, modes_k), F32)),
        0,
        partial,
        vol,
        modes,
        fast(surface_in),
        near_in,
        wrap_in,
        *raws[steps:],
    )
    shapes = (jax.ShapeDtypeStruct(adjoint.shape, F32), jax.ShapeDtypeStruct((1, modes_k), F32))
    residual, modal = call(final_kernel, "final", shapes, 0, partial, vol, line, mix, *last)
    return residual, modal


def solution(mesh):
    placed = (
        P("inst", None, "space", None, None),
        P("inst", None, None, None, "space", None, None),
        P("space", None, None),
        P("inst", None, "space", None, None),
        P(None, "space", None),
        P(None, "space", None),
        P("space", None),
        P(),
        P(),
    )
    return jax.shard_map(
        body,
        mesh=mesh,
        in_specs=placed,
        out_specs=(P("inst", None, "space", None, None), P("inst", None)),
        check_vma=False,
    )
```

```python
import functools
import math

import jax
import jax.numpy as jnp
import numpy as np
from jax import lax
from jax.experimental import pallas as pl
from jax.experimental.pallas import tpu as pltpu
from jax.sharding import PartitionSpec as P

VMEM = pl.BlockSpec(memory_space=pltpu.VMEM)
SMEM = pl.BlockSpec(memory_space=pltpu.SMEM)
ANY = pl.BlockSpec(memory_space=pl.ANY)
F32 = jnp.float32


def weight_values(count):
    table = []
    for k in range(count):
        if k == 0:
            first, second = 0.0, -(count * count + 2) / 12.0
        else:
            sign = 1.0 - 2.0 * (k % 2)
            sine = math.sin(math.pi * k / count)
            first = 0.5 * sign * math.cos(math.pi * k / count) / sine
            second = -0.5 * sign / (sine * sine)
        table.append(first - 0.25 * second)
    return np.asarray(table, np.float32)


def weight_of(count, source, target):
    gap = lax.rem(source - target + count, count)
    value = jnp.float32(0.0)
    for k, entry in enumerate(weight_values(count)):
        value = jnp.where(gap == k, jnp.float32(entry), value)
    return value


def raw_masks(count):
    steps = [mask for mask in range(2, count, 2) if mask & (mask - 1) == 0]
    others = [mask for mask in range(2, count, 2) if mask & (mask - 1)]
    first = [(steps[k], steps[(k + 1) % len(steps)]) for k in range(len(steps))]
    return first + [(mask + 1, mask + 1) for mask in others]


def held_masks(me):
    pairs = raw_masks(lax.axis_size("inst"))
    core = lax.rem(me, 2)
    return [0] + [jnp.where(core == a % 2, a, b) for a, b in pairs]


def table_kernel(out):
    me = lax.axis_index("inst")
    out[0, 0] = weight_of(lax.axis_size("inst"), me, me)


def hold_kernel(token, lam, out):
    out[...] = lam[...]


def prep_kernel(token, lam, outward, station, phi, inv_stiff, jac, near, wrap, packed, modes):
    nv, nx, ny, nz = lam.shape[1:]
    odd = lax.rem(lax.axis_index("space"), 2)

    def columns(j, carry):
        for minus, out in ((1 - odd, wrap), (odd, near)):
            plane = (nx - 1) * (1 - minus)
            total = jac[0, 1 + minus, 0, j, plane] * lam[0, 0, plane]
            for i in range(1, nv):
                total = total + jac[0, 1 + minus, i, j, plane] * lam[0, i, plane]
            out[pl.ds(pl.multiple_of(j * ny, ny), ny), :] = total
        return carry

    modes_k, stations = phi.shape
    full = phi[...]
    high = full.astype(jnp.bfloat16)
    rest = full - high.astype(F32)
    mid = rest.astype(jnp.bfloat16)
    low = (rest - mid.astype(F32)).astype(jnp.bfloat16)
    pieces = jnp.concatenate([low, mid, high], axis=0)
    rows = lax.broadcasted_iota(jnp.int32, (stations, nz), 0)
    share = jnp.zeros((modes_k, nz), F32)
    for x in range(nx):
        hot = (rows == station[x : x + 1, :]).astype(F32).astype(jnp.bfloat16)
        parts = jnp.dot(pieces, hot, preferred_element_type=F32)
        at_face = parts[:modes_k] + parts[modes_k : 2 * modes_k] + parts[2 * modes_k :]
        modes[x] = at_face
        face = outward[0, x : x + 1, :] * lam[0, 0, x, 0:1, :]
        for j in range(1, nv):
            face = face + outward[j, x : x + 1, :] * lam[0, j, x, 0:1, :]
        share = share + at_face * face
    lax.fori_loop(0, nv, columns, 0, unroll=True)
    row = lax.broadcasted_iota(jnp.int32, (modes_k, modes_k), 0)
    lane = lax.broadcasted_iota(jnp.int32, (modes_k, modes_k), 1)
    stiff = jnp.sum(jnp.where(row == lane, inv_stiff[...], 0.0), axis=1, keepdims=True)
    column = jnp.sum(share, axis=1, keepdims=True) * stiff
    tile_lane = lax.broadcasted_iota(jnp.int32, (8, nz), 1)
    tile = jnp.zeros((8, nz), F32)
    for group in range(modes_k // 8):
        tile = jnp.where(tile_lane == group, column[8 * group : 8 * group + 8], tile)
    packed[...] = tile
    near[nv * ny :, :] = tile
    wrap[nv * ny :, :] = tile


def mix_of(held, target, skip=0, core=0):
    count = lax.axis_size("inst")
    me = lax.axis_index("inst")
    there = me ^ core
    weights = [weight_of(count, there ^ mask, me ^ target) for mask in held_masks(there)[skip:]]
    return lambda j: sum(weight * block[0, j] for weight, block in zip(weights, held))


def share_kernel(partial, volume, *refs):
    held, (out, own) = refs[:-2], refs[-2:]
    there, here = mix_of(held, 1), mix_of(held, 0)

    def columns(j, carry):
        out[0, j] = there(j)
        own[0, j] = volume[...] * here(j) + partial[0, j]
        return carry

    lax.fori_loop(0, out.shape[1], columns, 0, unroll=True)


def flux_kernel(after, lam, source, jac, out):
    nv, nx, ny, nz = lam.shape[1:]
    y = lax.broadcasted_iota(jnp.int32, (ny, nz), 0)
    z = lax.broadcasted_iota(jnp.int32, (ny, nz), 1)

    def product(d, j, x):
        total = jac[0, d, 0, j, x] * lam[0, 0, x]
        for i in range(1, nv):
            total = total + jac[0, d, i, j, x] * lam[0, i, x]
        return total

    def columns(j, carry):
        for x in range(nx):
            total = product(0, j, x) - source[0, j, x]
            if x > 0:
                total = total + product(1, j, x - 1)
            if x < nx - 1:
                total = total + product(2, j, x + 1)
            total = total + jnp.where(y == 0, 0.0, pltpu.roll(product(3, j, x), 1, 0))
            total = total + jnp.where(y == ny - 1, 0.0, pltpu.roll(product(4, j, x), ny - 1, 0))
            total = total + jnp.where(z == 0, 0.0, pltpu.roll(product(5, j, x), 1, 1))
            total = total + jnp.where(z == nz - 1, 0.0, pltpu.roll(product(6, j, x), nz - 1, 1))
            out[0, j, x] = total
        return carry

    lax.fori_loop(0, nv, columns, 0, unroll=True)


def pick_kernel(packed, first, second, out):
    lower = lax.axis_index("space") < 2
    split = out.shape[0] - 8
    out[:split, :] = jnp.where(lower, first[:split, :], second[:split, :])
    out[split:, :] = packed[...] + first[split:, :] + second[split:, :]


def beam_kernel(partial, volume, modes, surface_in, near, wrap, *refs):
    held, (out, modal) = refs[:-2], refs[-2:]
    nv, nx, ny, nz = partial.shape[1:]
    groups = modal.shape[1] // 8
    own = mix_of(held, 0, len(held_masks(0)) - len(held))
    even = lax.rem(lax.axis_index("space"), 2) == 0
    tile = near[nv * ny :, :] + wrap[nv * ny :, :]
    columns = [tile[:, group : group + 1] for group in range(groups)]
    line = None
    for group, column in enumerate(columns):
        row = lax.broadcasted_iota(jnp.int32, (8, 8 * groups), 0)
        lane = lax.broadcasted_iota(jnp.int32, (8, 8 * groups), 1)
        piece = jnp.sum(jnp.where(lane == row + 8 * group, column, 0.0), axis=0, keepdims=True)
        line = piece if line is None else line + piece
    modal[...] = line
    low = lax.broadcasted_iota(jnp.int32, (ny, nz), 0) == 0
    backs = []
    for x in range(nx):
        back = jnp.zeros((8, nz), F32)
        for group, column in enumerate(columns):
            back = back + modes[x, 8 * group : 8 * group + 8, :] * column
        backs.append(jnp.sum(back, axis=0, keepdims=True))

    def step(j, carry):
        mixed = own(j)
        inward = surface_in[j]
        rows = pl.ds(pl.multiple_of(j * ny, ny), ny)
        first = jnp.where(even, wrap[rows, :], near[rows, :])
        last = jnp.where(even, near[rows, :], wrap[rows, :])
        for x in range(nx):
            value = partial[0, j, x] + volume[x] * mixed[x]
            if x == 0:
                value = value + first
            if x == nx - 1:
                value = value + last
            out[0, j, x] = value + jnp.where(low, inward[x : x + 1, :] * backs[x], 0.0)
        return carry

    lax.fori_loop(0, nv, step, 0, unroll=True)


def final_kernel(partial, volume, line, mix, *refs):
    last, (out, modal) = refs[:-2], refs[-2:]
    modal[...] = line[...]
    rest = mix_of(last, 0, len(held_masks(0)) - len(last), 1)

    def columns(j, carry):
        out[0, j] = partial[0, j] + volume[...] * (mix[0, j] + rest(j))
        return carry

    lax.fori_loop(0, out.shape[1], columns, 0, unroll=True)


def body(adjoint, jacobian, volume, source, surface_out, surface_in, station, phi, inv_stiff):
    count, slabs = lax.axis_size("inst"), lax.axis_size("space")
    nv, nx, ny, nz = adjoint.shape[1:]
    modes_k = phi.shape[0]

    def swap(value, axis, mask):
        size = lax.axis_size(axis)
        return lax.ppermute(value, axis, [(i, i ^ mask) for i in range(size)])

    def fast(array):
        return pltpu.with_memory_space_constraint(array, pltpu.VMEM)

    def call(kernel, name, out_shape, flops, *operands, specs=None):
        return pl.pallas_call(
            kernel,
            out_shape=out_shape,
            in_specs=[VMEM] * len(operands) if specs is None else specs,
            out_specs=jax.tree.map(lambda shape: SMEM if name == "table" else VMEM, out_shape),
            compiler_params=pltpu.CompilerParams(vmem_limit_bytes=4 * 2**20),
            cost_estimate=pl.CostEstimate(flops=flops, bytes_accessed=0, transcendentals=0),
            name=name,
        )(*operands)

    block = pltpu.VMEM(adjoint.shape, F32)
    steps = sum(mask & (mask - 1) == 0 for mask in range(2, count, 2))
    lam, jac = fast(adjoint), fast(jacobian)
    weights = call(table_kernel, "table", pltpu.SMEM((1, 1), F32), 2**33)
    held = call(hold_kernel, "hold", block, 0, weights, lam, specs=[SMEM, VMEM])
    raws = [
        lax.ppermute(adjoint if k < steps else held, "inst", [(i, i ^ pair[i % 2]) for i in range(count)])
        for k, pair in enumerate(raw_masks(count))
    ]
    rows = nv * ny + 8
    near, wrap, packed, modes = call(
        prep_kernel,
        "prep",
        (
            pltpu.VMEM((rows, nz), F32),
            pltpu.VMEM((rows, nz), F32),
            pltpu.VMEM((8, nz), F32),
            pltpu.VMEM((nx, modes_k, nz), F32),
        ),
        0,
        weights,
        lam,
        fast(surface_out),
        fast(station),
        fast(phi),
        fast(inv_stiff.reshape(1, modes_k)),
        jac,
        specs=[SMEM] + [VMEM] * 6,
    )
    if slabs == 4:
        first = lax.ppermute(wrap, "space", [(3, 0), (2, 1), (0, 2), (1, 3)])
        second = lax.ppermute(wrap, "space", [(0, 3), (1, 2), (2, 0), (3, 1)])
        near_in = swap(near, "space", 1)
        wrap_in = call(pick_kernel, "pick", pltpu.VMEM((rows, nz), F32), 2**31, packed, first, second)
    else:
        wrap_in = lax.ppermute(wrap, "space", [(i, (((i + 1) ^ 1) - 1) % slabs) for i in range(slabs)])
        near_in = swap(near, "space", 1)
        tile = packed + near_in[nv * ny :]
        step = 2
        while step < slabs:
            tile = tile + swap(tile, "space", step)
            step *= 2
        wrap_in = wrap_in.at[nv * ny :].set(tile)
        near_in = near_in.at[nv * ny :].set(0.0)
    partial = call(flux_kernel, "flux", block, 2 * jacobian.size, raws[0], lam, fast(source), jac, specs=[ANY] + [VMEM] * 3)
    vol = fast(volume)
    share, partial = call(share_kernel, "share", (block, block), 0, partial, vol, lam, *raws[:steps])
    mix = swap(share, "inst", 1)
    last = [swap(block, "inst", 1) for block in raws[steps:]]
    partial, line = call(
        beam_kernel,
        "beam",
        (block, pltpu.VMEM((1, modes_k), F32)),
        0,
        partial,
        vol,
        modes,
        fast(surface_in),
        near_in,
        wrap_in,
        *raws[steps:],
    )
    shapes = (jax.ShapeDtypeStruct(adjoint.shape, F32), jax.ShapeDtypeStruct((1, modes_k), F32))
    residual, modal = call(final_kernel, "final", shapes, 0, partial, vol, line, mix, *last)
    return residual, modal


def solution(mesh):
    placed = (
        P("inst", None, "space", None, None),
        P("inst", None, None, None, "space", None, None),
        P("space", None, None),
        P("inst", None, "space", None, None),
        P(None, "space", None),
        P(None, "space", None),
        P("space", None),
        P(),
        P(),
    )
    return jax.shard_map(
        body,
        mesh=mesh,
        in_specs=placed,
        out_specs=(P("inst", None, "space", None, None), P("inst", None)),
        check_vma=False,
    )
```

```python
import functools
import math

import jax
import jax.numpy as jnp
import numpy as np
from jax import lax
from jax.experimental import pallas as pl
from jax.experimental.pallas import tpu as pltpu
from jax.sharding import PartitionSpec as P

VMEM = pl.BlockSpec(memory_space=pltpu.VMEM)
SMEM = pl.BlockSpec(memory_space=pltpu.SMEM)
ANY = pl.BlockSpec(memory_space=pl.ANY)
F32 = jnp.float32


def weight_values(count):
    table = []
    for k in range(count):
        if k == 0:
            first, second = 0.0, -(count * count + 2) / 12.0
        else:
            sign = 1.0 - 2.0 * (k % 2)
            sine = math.sin(math.pi * k / count)
            first = 0.5 * sign * math.cos(math.pi * k / count) / sine
            second = -0.5 * sign / (sine * sine)
        table.append(first - 0.25 * second)
    return np.asarray(table, np.float32)


def weight_of(count, source, target):
    gap = lax.rem(source - target + count, count)
    value = jnp.float32(0.0)
    for k, entry in enumerate(weight_values(count)):
        value = jnp.where(gap == k, jnp.float32(entry), value)
    return value


def raw_masks(count):
    steps = [mask for mask in range(2, count, 2) if mask & (mask - 1) == 0]
    others = [mask for mask in range(2, count, 2) if mask & (mask - 1)]
    first = [(steps[k], steps[(k + 1) % len(steps)]) for k in range(len(steps))]
    return first + [(mask + 1, mask + 1) for mask in others]


def held_masks(me):
    pairs = raw_masks(lax.axis_size("inst"))
    core = lax.rem(me, 2)
    return [0] + [jnp.where(core == a % 2, a, b) for a, b in pairs]


def table_kernel(out):
    me = lax.axis_index("inst")
    out[0, 0] = weight_of(lax.axis_size("inst"), me, me)


def hold_kernel(token, lam, out):
    out[...] = lam[...]


def prep_kernel(token, lam, outward, station, phi, inv_stiff, jac, near, wrap, packed, modes):
    nv, nx, ny, nz = lam.shape[1:]
    odd = lax.rem(lax.axis_index("space"), 2)

    def columns(j, carry):
        for minus, out in ((1 - odd, wrap), (odd, near)):
            plane = (nx - 1) * (1 - minus)
            total = jac[0, 1 + minus, 0, j, plane] * lam[0, 0, plane]
            for i in range(1, nv):
                total = total + jac[0, 1 + minus, i, j, plane] * lam[0, i, plane]
            out[pl.ds(pl.multiple_of(j * ny, ny), ny), :] = total
        return carry

    modes_k, stations = phi.shape
    row = lax.broadcasted_iota(jnp.int32, (modes_k, modes_k), 0)
    lane = lax.broadcasted_iota(jnp.int32, (modes_k, modes_k), 1)
    stiff = jnp.sum(jnp.where(row == lane, inv_stiff[...], 0.0), axis=1, keepdims=True)
    full = phi[...]
    high = full.astype(jnp.bfloat16)
    rest = full - high.astype(F32)
    mid = rest.astype(jnp.bfloat16)
    low = (rest - mid.astype(F32)).astype(jnp.bfloat16)
    pieces = jnp.concatenate([low, mid, high], axis=0)
    rows = lax.broadcasted_iota(jnp.int32, (stations, nz), 0)
    share = jnp.zeros((modes_k, nz), F32)
    for x in range(nx):
        hot = (rows == station[x : x + 1, :]).astype(F32).astype(jnp.bfloat16)
        parts = jnp.dot(pieces, hot, preferred_element_type=F32)
        at_face = parts[:modes_k] + parts[modes_k : 2 * modes_k] + parts[2 * modes_k :]
        modes[x] = at_face
        face = outward[0, x : x + 1, :] * lam[0, 0, x, 0:1, :]
        for j in range(1, nv):
            face = face + outward[j, x : x + 1, :] * lam[0, j, x, 0:1, :]
        share = share + at_face * face
    lax.fori_loop(0, nv, columns, 0, unroll=True)
    column = jnp.sum(share, axis=1, keepdims=True) * stiff
    tile_lane = lax.broadcasted_iota(jnp.int32, (8, nz), 1)
    tile = jnp.zeros((8, nz), F32)
    for group in range(modes_k // 8):
        tile = jnp.where(tile_lane == group, column[8 * group : 8 * group + 8], tile)
    packed[...] = tile
    near[nv * ny :, :] = tile
    wrap[nv * ny :, :] = tile


def mix_of(held, target, skip=0, core=0):
    count = lax.axis_size("inst")
    me = lax.axis_index("inst")
    there = me ^ core
    weights = [weight_of(count, there ^ mask, me ^ target) for mask in held_masks(there)[skip:]]
    return lambda j: sum(weight * block[0, j] for weight, block in zip(weights, held))


def share_kernel(partial, volume, *refs):
    held, (out, own) = refs[:-2], refs[-2:]
    there, here = mix_of(held, 1), mix_of(held, 0)

    def columns(j, carry):
        out[0, j] = there(j)
        own[0, j] = volume[...] * here(j) + partial[0, j]
        return carry

    lax.fori_loop(0, out.shape[1], columns, 0, unroll=True)


def flux_kernel(after, lam, source, jac, out):
    nv, nx, ny, nz = lam.shape[1:]
    y = lax.broadcasted_iota(jnp.int32, (ny, nz), 0)
    z = lax.broadcasted_iota(jnp.int32, (ny, nz), 1)

    def product(d, j, x):
        total = jac[0, d, 0, j, x] * lam[0, 0, x]
        for i in range(1, nv):
            total = total + jac[0, d, i, j, x] * lam[0, i, x]
        return total

    def columns(j, carry):
        for x in range(nx):
            total = product(0, j, x) - source[0, j, x]
            if x > 0:
                total = total + product(1, j, x - 1)
            if x < nx - 1:
                total = total + product(2, j, x + 1)
            total = total + jnp.where(y == 0, 0.0, pltpu.roll(product(3, j, x), 1, 0))
            total = total + jnp.where(y == ny - 1, 0.0, pltpu.roll(product(4, j, x), ny - 1, 0))
            total = total + jnp.where(z == 0, 0.0, pltpu.roll(product(5, j, x), 1, 1))
            total = total + jnp.where(z == nz - 1, 0.0, pltpu.roll(product(6, j, x), nz - 1, 1))
            out[0, j, x] = total
        return carry

    lax.fori_loop(0, nv, columns, 0, unroll=True)


def pick_kernel(packed, first, second, out):
    lower = lax.axis_index("space") < 2
    split = out.shape[0] - 8
    out[:split, :] = jnp.where(lower, first[:split, :], second[:split, :])
    out[split:, :] = packed[...] + first[split:, :] + second[split:, :]


def beam_kernel(partial, volume, modes, surface_in, near, wrap, *refs):
    held, (out, modal) = refs[:-2], refs[-2:]
    nv, nx, ny, nz = partial.shape[1:]
    groups = modal.shape[1] // 8
    own = mix_of(held, 0, len(held_masks(0)) - len(held))
    even = lax.rem(lax.axis_index("space"), 2) == 0
    tile = near[nv * ny :, :] + wrap[nv * ny :, :]
    columns = [tile[:, group : group + 1] for group in range(groups)]
    line = None
    for group, column in enumerate(columns):
        row = lax.broadcasted_iota(jnp.int32, (8, 8 * groups), 0)
        lane = lax.broadcasted_iota(jnp.int32, (8, 8 * groups), 1)
        piece = jnp.sum(jnp.where(lane == row + 8 * group, column, 0.0), axis=0, keepdims=True)
        line = piece if line is None else line + piece
    modal[...] = line
    low = lax.broadcasted_iota(jnp.int32, (ny, nz), 0) == 0
    backs = []
    for x in range(nx):
        back = jnp.zeros((8, nz), F32)
        for group, column in enumerate(columns):
            back = back + modes[x, 8 * group : 8 * group + 8, :] * column
        backs.append(jnp.sum(back, axis=0, keepdims=True))

    def step(j, carry):
        mixed = own(j)
        inward = surface_in[j]
        rows = pl.ds(pl.multiple_of(j * ny, ny), ny)
        first = jnp.where(even, wrap[rows, :], near[rows, :])
        last = jnp.where(even, near[rows, :], wrap[rows, :])
        for x in range(nx):
            value = partial[0, j, x] + volume[x] * mixed[x]
            if x == 0:
                value = value + first
            if x == nx - 1:
                value = value + last
            out[0, j, x] = value + jnp.where(low, inward[x : x + 1, :] * backs[x], 0.0)
        return carry

    lax.fori_loop(0, nv, step, 0, unroll=True)


def final_kernel(partial, volume, line, mix, *refs):
    last, (out, modal) = refs[:-2], refs[-2:]
    modal[...] = line[...]
    rest = mix_of(last, 0, len(held_masks(0)) - len(last), 1)

    def columns(j, carry):
        out[0, j] = partial[0, j] + volume[...] * (mix[0, j] + rest(j))
        return carry

    lax.fori_loop(0, out.shape[1], columns, 0, unroll=True)


def body(adjoint, jacobian, volume, source, surface_out, surface_in, station, phi, inv_stiff):
    count, slabs = lax.axis_size("inst"), lax.axis_size("space")
    nv, nx, ny, nz = adjoint.shape[1:]
    modes_k = phi.shape[0]

    def swap(value, axis, mask):
        size = lax.axis_size(axis)
        return lax.ppermute(value, axis, [(i, i ^ mask) for i in range(size)])

    def fast(array):
        return pltpu.with_memory_space_constraint(array, pltpu.VMEM)

    def call(kernel, name, out_shape, flops, *operands, specs=None):
        return pl.pallas_call(
            kernel,
            out_shape=out_shape,
            in_specs=[VMEM] * len(operands) if specs is None else specs,
            out_specs=jax.tree.map(lambda shape: SMEM if name == "table" else VMEM, out_shape),
            compiler_params=pltpu.CompilerParams(vmem_limit_bytes=4 * 2**20),
            cost_estimate=pl.CostEstimate(flops=flops, bytes_accessed=0, transcendentals=0),
            name=name,
        )(*operands)

    block = pltpu.VMEM(adjoint.shape, F32)
    steps = sum(mask & (mask - 1) == 0 for mask in range(2, count, 2))
    lam, jac = fast(adjoint), fast(jacobian)
    weights = call(table_kernel, "table", pltpu.SMEM((1, 1), F32), 2**33)
    held = call(hold_kernel, "hold", block, 0, weights, lam, specs=[SMEM, VMEM])
    raws = [
        lax.ppermute(adjoint if k < steps else held, "inst", [(i, i ^ pair[i % 2]) for i in range(count)])
        for k, pair in enumerate(raw_masks(count))
    ]
    rows = nv * ny + 8
    near, wrap, packed, modes = call(
        prep_kernel,
        "prep",
        (
            pltpu.VMEM((rows, nz), F32),
            pltpu.VMEM((rows, nz), F32),
            pltpu.VMEM((8, nz), F32),
            pltpu.VMEM((nx, modes_k, nz), F32),
        ),
        0,
        weights,
        lam,
        fast(surface_out),
        fast(station),
        fast(phi),
        fast(inv_stiff.reshape(1, modes_k)),
        jac,
        specs=[SMEM] + [VMEM] * 6,
    )
    if slabs == 4:
        first = lax.ppermute(wrap, "space", [(3, 0), (2, 1), (0, 2), (1, 3)])
        second = lax.ppermute(wrap, "space", [(0, 3), (1, 2), (2, 0), (3, 1)])
        near_in = swap(near, "space", 1)
        wrap_in = call(pick_kernel, "pick", pltpu.VMEM((rows, nz), F32), 2**31, packed, first, second)
    else:
        wrap_in = lax.ppermute(wrap, "space", [(i, (((i + 1) ^ 1) - 1) % slabs) for i in range(slabs)])
        near_in = swap(near, "space", 1)
        tile = packed + near_in[nv * ny :]
        step = 2
        while step < slabs:
            tile = tile + swap(tile, "space", step)
            step *= 2
        wrap_in = wrap_in.at[nv * ny :].set(tile)
        near_in = near_in.at[nv * ny :].set(0.0)
    partial = call(flux_kernel, "flux", block, 2 * jacobian.size, raws[0], lam, fast(source), jac, specs=[ANY] + [VMEM] * 3)
    vol = fast(volume)
    share, partial = call(share_kernel, "share", (block, block), 0, partial, vol, lam, *raws[:steps])
    mix = swap(share, "inst", 1)
    last = [swap(block, "inst", 1) for block in raws[steps:]]
    partial, line = call(
        beam_kernel,
        "beam",
        (block, pltpu.VMEM((1, modes_k), F32)),
        0,
        partial,
        vol,
        modes,
        fast(surface_in),
        near_in,
        wrap_in,
        *raws[steps:],
    )
    shapes = (jax.ShapeDtypeStruct(adjoint.shape, F32), jax.ShapeDtypeStruct((1, modes_k), F32))
    residual, modal = call(final_kernel, "final", shapes, 0, partial, vol, line, mix, *last)
    return residual, modal


def solution(mesh):
    placed = (
        P("inst", None, "space", None, None),
        P("inst", None, None, None, "space", None, None),
        P("space", None, None),
        P("inst", None, "space", None, None),
        P(None, "space", None),
        P(None, "space", None),
        P("space", None),
        P(),
        P(),
    )
    return jax.shard_map(
        body,
        mesh=mesh,
        in_specs=placed,
        out_specs=(P("inst", None, "space", None, None), P("inst", None)),
        check_vma=False,
    )
```
